512 devices in a mesh: pi: 2 (over y_hi), pj: 8 (over y_lo, core), pix: 32 (over z, x).
Axes of the slice: x: 4, y: 8 (y_hi: 2, y_lo: 4; y = y_hi * 4 + y_lo), z: 8, core: 2. Of those that a mesh axis runs over, the one named last changes fastest.
Arguments:
- images: bfloat16 [2, 64, 512, 128], P(None, ('pi', 'pj'), 'pix'), may hold values from -3.01 to 3.01, as said below
Outputs:
- coherence: bfloat16 [64, 64, 512, 128], P('pi', 'pj', 'pix')
The draws below stay inside these ranges and needn't reach their ends.
Inputs may be any that keep to these rules, and one draw needn't show every extreme that they name: `images`: every complex entry has magnitude between 0.29 and 3.01.
All inputs are finite; a program needn't handle non-finite values.
Results may differ from the reference program's by a relative error of at most 0.001.
Values may be sent and summed in bfloat16 or wider, within the bound.
A program may use at most 64 MiB of HBM per device.

```python
import math
import jax
import jax.numpy as jnp
from jax import lax

P_SIZE = 64
COLS = 128
ROWS = 512


def draw_images(key, part):
    key = jax.random.fold_in(key, 11)
    keys = jax.random.split(key, 5)
    scene = jax.random.uniform(keys[0], (ROWS, COLS), jnp.float32, -math.pi, math.pi)
    spread = jnp.exp(jax.random.uniform(keys[1], (ROWS, COLS), jnp.float32, math.log(0.15), math.log(2.5)))
    factor = jnp.exp(jax.random.uniform(keys[2], (P_SIZE, 1, 1), jnp.float32, math.log(0.5), math.log(2.0)))
    noise = jax.random.uniform(keys[3], (P_SIZE, ROWS, COLS), jnp.float32, -1.0, 1.0)
    phase = scene[None] + spread[None] * factor * noise * math.pi
    amplitude = jnp.exp(jax.random.uniform(keys[4], (P_SIZE, ROWS, COLS), jnp.float32, math.log(0.3), math.log(3.0)))
    result = jnp.stack([amplitude * jnp.cos(phase), amplitude * jnp.sin(phase)])
    return result.astype(jnp.bfloat16)


def setup_inputs(seed: int = 0) -> dict:
    splits = jax.random.split(jax.random.key(seed), 2)
    return {
        "images": draw_images(jax.random.fold_in(splits[1], 71), 0),
    }


def box_sum(values, axis):
    pad_width = [(0, 0)] * values.ndim
    pad_width[axis] = (3, 3)
    padded = jnp.pad(values, pad_width)
    length = values.shape[axis]
    total = lax.slice_in_dim(padded, 0, length, axis=axis)
    for offset in range(1, 7):
        total = total + lax.slice_in_dim(padded, offset, offset + length, axis=axis)
    return total

def reference(images):
    data = images.astype(jnp.float32)
    real_all = data[0]
    imag_all = data[1]
    power = box_sum(box_sum(real_all * real_all + imag_all * imag_all, 1), 2)

    def one_pass(index):
        first_real = real_all[index]
        first_imag = imag_all[index]
        cross_real = first_real * real_all + first_imag * imag_all
        cross_imag = first_imag * real_all - first_real * imag_all
        sum_real = box_sum(box_sum(cross_real, 1), 2)
        sum_imag = box_sum(box_sum(cross_imag, 1), 2)
        magnitude = jnp.sqrt(sum_real * sum_real + sum_imag * sum_imag) * lax.rsqrt(power[index] * power)
        return magnitude.astype(jnp.bfloat16)
    return lax.map(one_pass, jnp.arange(P_SIZE, dtype=jnp.int32))
```

```python
import jax
import jax.numpy as jnp
from jax import lax
from jax.experimental import pallas as pl
from jax.experimental.pallas import tpu as pltpu
from jax.sharding import PartitionSpec as P

BF = jnp.bfloat16
F32 = jnp.float32
MESH = pl.DeviceIdType.MESH
WINDOW = 22
COLS = 128
MATES = 8
UNROLL = 4


def table_row(group, part, row):
    return ((group * 2 + part) * WINDOW + row) * 8


def sum_seven(x):
    pairs = {j: x[j] + x[j + 1] for j in range(1, 20, 2)}
    out = []
    for i in range(0, 16, 2):
        middle = pairs[i + 1] + pairs[i + 3] + pairs[i + 5]
        out.append(x[i] + middle)
        out.append(middle + x[i + 7])
    return out


def sum_columns(rows, band):
    x = jnp.concatenate(rows, axis=0)
    high = x.astype(BF)
    low = (x - high.astype(F32)).astype(BF)
    return jnp.dot(jnp.concatenate([high, low], axis=1), band, preferred_element_type=F32)


def band_matrix():
    r = lax.broadcasted_iota(jnp.int32, (COLS, COLS), 0)
    c = lax.broadcasted_iota(jnp.int32, (COLS, COLS), 1)
    band = jnp.where(jnp.abs(r - c) <= 3, 1.0, 0.0).astype(BF)
    return jnp.concatenate([band, band], axis=0)


def spread_image(block, table, group, half):
    for part in range(2):
        for p in range(4):
            rows = block[part, p].astype(F32)
            for j in range(2):
                start = table_row(group, part, 3 + 8 * j) + half * 4 + p
                table[pl.ds(start, 8, stride=8), :] = rows[8 * j : 8 * j + 8]


def spread_halo(halo, table, group, half, pix, last):
    for edge in range(2):
        outside = (pix == 0) if edge == 0 else (pix == last)
        rows = jnp.where(outside, 0.0, halo[edge].astype(F32))
        for part in range(2):
            for k in range(3):
                start = table_row(group, part, (0 if edge == 0 else 19) + k) + half * 4
                table[pl.ds(start, 4), :] = rows[(part * 3 + k) * 4 : (part * 3 + k) * 4 + 4]


def inverse_root_power(table, scale, group, band):
    power = []
    for k in range(WINDOW):
        a = table[pl.ds(table_row(group, 0, k), 8), :]
        b = table[pl.ds(table_row(group, 1, k), 8), :]
        power.append(a * a + b * b)
    scale[pl.ds(group * 128, 128), :] = lax.rsqrt(sum_columns(sum_seven(power), band))


def coherence_of(m, second, table, scale, stage, out, band):
    group, s = m // 8, m % 8
    real, imag = [], []
    for k in range(WINDOW):
        a = jnp.broadcast_to(table[pl.ds(table_row(group, 0, k) + s, 1), :], (8, COLS))
        b = jnp.broadcast_to(table[pl.ds(table_row(group, 1, k) + s, 1), :], (8, COLS))
        c = table[pl.ds(table_row(second, 0, k), 8), :]
        d = table[pl.ds(table_row(second, 1, k), 8), :]
        real.append(a * c + b * d)
        imag.append(b * c - a * d)
    w = sum_columns(sum_seven(real) + sum_seven(imag), band)
    for r in range(16):
        x = w[r * 8 : r * 8 + 8]
        y = w[128 + r * 8 : 128 + r * 8 + 8]
        q = x * x + y * y
        first = jnp.broadcast_to(scale[pl.ds(group * 128 + r * 8 + s, 1), :], (8, COLS))
        other = scale[pl.ds(second * 128 + r * 8, 8), :]
        value = (q * lax.rsqrt(jnp.maximum(q, 1e-36))) * (first * other)
        stage[pl.ds(r, 8, stride=16), :] = value
    for n in range(8):
        out[m, n] = stage[pl.ds(n * 16, 16), :].astype(BF)


def kernel(images, out, blocks, halos, edges, edge_rows, table, scale, stage,
           pix_send, pix_recv, block_send, block_recv, halo_send, halo_recv):
    pi, pj, pix = lax.axis_index("pi"), lax.axis_index("pj"), lax.axis_index("pix")
    strips = lax.axis_size("pix")
    up, down = lax.rem(pix + strips - 1, strips), lax.rem(pix + 1, strips)
    far = (pj // 4) != pi
    barrier = pltpu.get_barrier_semaphore()
    for strip in (up, down):
        pl.semaphore_signal(barrier, inc=1, device_id={"pix": strip}, device_id_type=MESH)
    for off in range(1, MATES):
        pl.semaphore_signal(barrier, inc=1, device_id={"pj": lax.rem(pj + off, MATES)}, device_id_type=MESH)

    @pl.when(far)
    def _():
        for core in range(2):
            pl.semaphore_signal(
                barrier, inc=1, device_id={"pi": 1 - pi, "pj": 2 * lax.rem(pj, 4) + core}, device_id_type=MESH
            )

    spread_image(images, table, pj // 2, lax.rem(pj, 2))
    blocks[pj] = images[...]
    edge_rows[...] = jnp.zeros_like(edge_rows)
    for edge in range(2):
        for part in range(2):
            for k in range(3):
                start = table_row(pj // 2, part, (3 if edge == 0 else 16) + k) + lax.rem(pj, 2) * 4
                edge_rows[edge, pl.ds((part * 3 + k) * 4, 4), :] = table[pl.ds(start, 4), :]
    edges[...] = edge_rows[...].astype(BF)
    band = band_matrix()

    pl.semaphore_wait(barrier, 2 + (MATES - 1) + 1)

    to_strips = []
    for edge, strip in ((0, up), (1, down)):
        copy = pltpu.make_async_remote_copy(
            src_ref=edges.at[edge], dst_ref=halos.at[pj, 1 - edge], send_sem=pix_send.at[edge],
            recv_sem=pix_recv.at[1 - edge], device_id={"pix": strip}, device_id_type=MESH)
        copy.start()
        to_strips.append(copy)

    far_target = {"pi": 1 - pi, "pj": 4 * pi + pj // 2}

    def sends(source, place, send_sem, recv_sem):
        copies = []
        copies.append(pltpu.make_async_remote_copy(
            src_ref=source, dst_ref=place.at[MATES + lax.rem(pj, 2)], send_sem=send_sem.at[0],
            recv_sem=recv_sem.at[MATES + lax.rem(pj, 2)], device_id=far_target, device_id_type=MESH))
        for off in range(1, MATES):
            copies.append(pltpu.make_async_remote_copy(
                src_ref=source, dst_ref=place.at[pj], send_sem=send_sem.at[off],
                recv_sem=recv_sem.at[pj], device_id={"pj": lax.rem(pj + off, MATES)}, device_id_type=MESH))
        for copy in copies:
            copy.start()
        return copies

    block_copies = sends(images, blocks, block_send, block_recv)
    for copy in to_strips:
        copy.wait()
    halo_copies = sends(halos.at[pj], halos, halo_send, halo_recv)

    def arrived(slot):
        def wait(place, sem):
            pltpu.make_async_remote_copy(
                src_ref=place.at[slot], dst_ref=place.at[slot], send_sem=sem.at[slot], recv_sem=sem.at[slot],
                device_id={"pj": lax.rem(pj + 1, MATES)}, device_id_type=MESH).wait_recv()
        wait(blocks, block_recv)
        wait(halos, halo_recv)

    def take(group):
        def one(half, _):
            slot = group * 2 + half

            @pl.when(slot != pj)
            def _():
                arrived(slot)

            spread_image(blocks.at[slot], table, group, half)
            spread_halo(halos.at[slot], table, group, half, pix, strips - 1)
            return 0

        lax.fori_loop(0, 2, one, 0)
        inverse_root_power(table, scale, group, band)

    @pl.when(far)
    def _():
        take(MATES // 2)

    second = jnp.where(far, MATES // 2, lax.rem(pj, 4))
    start = jnp.where(far, pj // 2, lax.rem(pj, 4))

    def step(i, _):
        group = lax.rem(start + i, 4)
        take(group)

        def one(s, _):
            coherence_of(group * 8 + s, second, table, scale, stage, out, band)
            return 0

        lax.fori_loop(0, 8, one, 0, unroll=UNROLL)
        return 0

    lax.fori_loop(0, 4, step, 0)
    for copy in block_copies + halo_copies:
        copy.wait_send()


def per_device(images):
    return pl.pallas_call(
        kernel,
        out_shape=pltpu.VMEM((32, 8, 16, COLS), BF),
        in_specs=[pl.BlockSpec(memory_space=pltpu.VMEM)],
        out_specs=pl.BlockSpec(memory_space=pltpu.VMEM),
        scratch_shapes=[
            pltpu.VMEM((MATES + 2, 2, 4, 16, COLS), BF),
            pltpu.VMEM((MATES + 2, 2, 32, COLS), BF),
            pltpu.VMEM((2, 32, COLS), BF),
            pltpu.VMEM((2, 32, COLS), F32),
            pltpu.VMEM((5 * 2 * WINDOW * 8, COLS), F32),
            pltpu.VMEM((5 * 128, COLS), F32),
            pltpu.VMEM((128, COLS), F32),
            pltpu.SemaphoreType.DMA((2,)),
            pltpu.SemaphoreType.DMA((2,)),
            pltpu.SemaphoreType.DMA((MATES,)),
            pltpu.SemaphoreType.DMA((MATES + 2,)),
            pltpu.SemaphoreType.DMA((MATES,)),
            pltpu.SemaphoreType.DMA((MATES + 2,)),
        ],
        compiler_params=pltpu.CompilerParams(
            collective_id=0, has_side_effects=True, vmem_limit_bytes=24 << 20
        ),
        name="coherence",
    )(images)


def solution(mesh):
    return jax.shard_map(
        per_device,
        mesh=mesh,
        in_specs=(P(None, ("pi", "pj"), "pix", None),),
        out_specs=P("pi", "pj", "pix", None),
        check_vma=False,
    )
```

```python
import jax
import jax.numpy as jnp
from jax import lax
from jax.experimental import pallas as pl
from jax.experimental.pallas import tpu as pltpu
from jax.sharding import PartitionSpec as P

BF = jnp.bfloat16
F32 = jnp.float32
MESH = pl.DeviceIdType.MESH
WINDOW = 22
COLS = 128
MATES = 8
EDGE = 24
UNROLL = 4


def table_row(group, part, row):
    return ((group * 2 + part) * WINDOW + row) * 8


def sum_seven(x):
    pairs = {j: x[j] + x[j + 1] for j in range(1, 20, 2)}
    out = []
    for i in range(0, 16, 2):
        middle = pairs[i + 1] + pairs[i + 3] + pairs[i + 5]
        out.append(x[i] + middle)
        out.append(middle + x[i + 7])
    return out


def sum_columns(rows, band):
    x = jnp.concatenate(rows, axis=0)
    high = x.astype(BF)
    low = (x - high.astype(F32)).astype(BF)
    return jnp.dot(jnp.concatenate([high, low], axis=1), band, preferred_element_type=F32)


def band_matrix():
    r = lax.broadcasted_iota(jnp.int32, (COLS, COLS), 0)
    c = lax.broadcasted_iota(jnp.int32, (COLS, COLS), 1)
    band = jnp.where(jnp.abs(r - c) <= 3, 1.0, 0.0).astype(BF)
    return jnp.concatenate([band, band], axis=0)


def spread_image(block, table, group, half):
    for part in range(2):
        for p in range(4):
            rows = block[part, p].astype(F32)
            for j in range(2):
                start = table_row(group, part, 3 + 8 * j) + half * 4 + p
                table[pl.ds(start, 8, stride=8), :] = rows[8 * j : 8 * j + 8]


def spread_halo(halo, table, group, half):
    rows = halo[...].astype(F32)
    for edge in range(2):
        for part in range(2):
            for k in range(3):
                start = table_row(group, part, (0 if edge == 0 else 19) + k) + half * 4
                first = EDGE * edge + (part * 3 + k) * 4
                table[pl.ds(start, 4), :] = rows[first : first + 4]


def inverse_root_power(table, scale, group, band):
    power = []
    for k in range(WINDOW):
        a = table[pl.ds(table_row(group, 0, k), 8), :]
        b = table[pl.ds(table_row(group, 1, k), 8), :]
        power.append(a * a + b * b)
    scale[pl.ds(group * 128, 128), :] = lax.rsqrt(sum_columns(sum_seven(power), band))


def coherence_of(m, second, table, scale, stage, out, band):
    group, s = m // 8, m % 8
    real, imag = [], []
    for k in range(WINDOW):
        a = jnp.broadcast_to(table[pl.ds(table_row(group, 0, k) + s, 1), :], (8, COLS))
        b = jnp.broadcast_to(table[pl.ds(table_row(group, 1, k) + s, 1), :], (8, COLS))
        c = table[pl.ds(table_row(second, 0, k), 8), :]
        d = table[pl.ds(table_row(second, 1, k), 8), :]
        real.append(a * c + b * d)
        imag.append(b * c - a * d)
    w = sum_columns(sum_seven(real) + sum_seven(imag), band)
    for r in range(16):
        x = w[r * 8 : r * 8 + 8]
        y = w[128 + r * 8 : 128 + r * 8 + 8]
        q = x * x + y * y
        first = jnp.broadcast_to(scale[pl.ds(group * 128 + r * 8 + s, 1), :], (8, COLS))
        other = scale[pl.ds(second * 128 + r * 8, 8), :]
        value = (q * lax.rsqrt(jnp.maximum(q, 1e-36))) * (first * other)
        stage[pl.ds(r, 8, stride=16), :] = value
    for n in range(8):
        out[m, n] = stage[pl.ds(n * 16, 16), :].astype(BF)


def kernel(images, out, own, blocks, halos, edges, from_strips, edge_rows, table, scale, stage,
           own_sem, pix_send, pix_recv, block_send, block_recv, pass_send, halo_send, halo_recv):
    pi, pj, pix = lax.axis_index("pi"), lax.axis_index("pj"), lax.axis_index("pix")
    last = lax.axis_size("pix") - 1
    chip, core = pj // 2, lax.rem(pj, 2)
    far = (pj // 4) != pi
    not_first, not_last = pix > 0, pix < last

    def mate(chips, cores=0):
        return {"pj": 2 * lax.rem(chip + chips, 4) + lax.rem(core + cores, 2)}

    mates = [mate(3, 0), mate(3, 1), mate(2, 0), mate(2, 1), mate(1, 0), mate(1, 1), mate(0, 1)]
    far_target = {"pi": 1 - pi, "pj": 4 * pi + chip}

    fetch = pltpu.make_async_copy(images, own, own_sem)
    fetch.start()
    barrier = pltpu.get_barrier_semaphore()

    def greet(device):
        pl.semaphore_signal(barrier, inc=1, device_id=device, device_id_type=MESH)

    @pl.when(far)
    def _():
        for c in range(2):
            greet({"pi": 1 - pi, "pj": 2 * lax.rem(pj, 4) + c})

    for device in mates:
        greet(device)

    @pl.when(not_first)
    def _():
        greet({"pix": pix - 1})

    @pl.when(not_last)
    def _():
        greet({"pix": pix + 1})

    band = band_matrix()
    fetch.wait()
    spread_image(own, table, chip, core)
    edge_rows[...] = jnp.zeros_like(edge_rows)
    for edge in range(2):
        for part in range(2):
            for k in range(3):
                start = table_row(chip, part, (3 if edge == 0 else 16) + k) + core * 4
                edge_rows[edge, pl.ds((part * 3 + k) * 4, 4), :] = table[pl.ds(start, 4), :]
    edges[...] = edge_rows[...].astype(BF)

    pl.semaphore_wait(barrier, MATES + not_first.astype(jnp.int32) + not_last.astype(jnp.int32))

    def to_strip(edge, strip):
        return pltpu.make_async_remote_copy(
            src_ref=edges.at[edge], dst_ref=from_strips.at[1 - edge], send_sem=pix_send.at[edge],
            recv_sem=pix_recv.at[1 - edge], device_id={"pix": strip}, device_id_type=MESH)

    def send(source, place, slot, send_sem, recv_sem, device):
        copy = pltpu.make_async_remote_copy(
            src_ref=source, dst_ref=place.at[slot], send_sem=send_sem,
            recv_sem=recv_sem.at[slot], device_id=device, device_id_type=MESH)
        copy.start()
        return copy

    @pl.when(not_first)
    def _():
        to_strip(0, pix - 1).start()

    @pl.when(not_last)
    def _():
        to_strip(1, pix + 1).start()

    sent = [send(own, blocks, MATES + core, block_send.at[0], block_recv, far_target)]
    for i, device in enumerate((mate(3), mate(2), mate(1), mate(0, 1))):
        sent.append(send(own, blocks, pj, block_send.at[1 + i], block_recv, device))

    @pl.when(not_first)
    def _():
        to_strip(1, pix - 1).wait_recv()

    @pl.when(not_last)
    def _():
        to_strip(0, pix + 1).wait_recv()

    @pl.when(jnp.logical_not(not_first))
    def _():
        from_strips[0] = jnp.zeros((32, COLS), BF)

    @pl.when(jnp.logical_not(not_last))
    def _():
        from_strips[1] = jnp.zeros((32, COLS), BF)

    both = jnp.concatenate([from_strips[edge].astype(F32)[:EDGE] for edge in range(2)], axis=0)
    halos[pj] = both.astype(BF)
    sent.append(send(halos.at[pj], halos, MATES + core, halo_send.at[0], halo_recv, far_target))
    for i, device in enumerate(mates):
        sent.append(send(halos.at[pj], halos, pj, halo_send.at[1 + i], halo_recv, device))

    def arrived(slot, place, sem):
        pltpu.make_async_remote_copy(
            src_ref=place.at[slot], dst_ref=place.at[slot], send_sem=sem.at[slot], recv_sem=sem.at[slot],
            device_id=mate(0, 1), device_id_type=MESH).wait_recv()

    for i in range(1, 4):
        slot = 2 * lax.rem(chip + i, 4) + core
        arrived(slot, blocks, block_recv)
        sent.append(send(blocks.at[slot], blocks, slot, pass_send.at[i], block_recv, mate(0, 1)))

    def take(group):
        def one(half, _):
            slot = group * 2 + half

            @pl.when(slot != pj)
            def _():
                @pl.when(jnp.logical_or(half != core, group == MATES // 2))
                def _():
                    arrived(slot, blocks, block_recv)

                spread_image(blocks.at[slot], table, group, half)
                arrived(slot, halos, halo_recv)

            spread_halo(halos.at[slot], table, group, half)
            return 0

        lax.fori_loop(0, 2, one, 0)
        inverse_root_power(table, scale, group, band)

    second = jnp.where(far, MATES // 2, lax.rem(pj, 4))
    take(second)

    def step(i, _):
        group = lax.rem(chip + i, 4)

        @pl.when(group != second)
        def _():
            take(group)

        def one(s, _):
            coherence_of(group * 8 + s, second, table, scale, stage, out, band)
            return 0

        lax.fori_loop(0, 8, one, 0, unroll=UNROLL)
        return 0

    lax.fori_loop(0, 4, step, 0)
    for copy in sent:
        copy.wait_send()

    @pl.when(not_first)
    def _():
        to_strip(0, pix - 1).wait_send()

    @pl.when(not_last)
    def _():
        to_strip(1, pix + 1).wait_send()


def per_device(images):
    return pl.pallas_call(
        kernel,
        out_shape=pltpu.VMEM((32, 8, 16, COLS), BF),
        in_specs=[pl.BlockSpec(memory_space=pltpu.HBM)],
        out_specs=pl.BlockSpec(memory_space=pltpu.VMEM),
        scratch_shapes=[
            pltpu.VMEM((2, 4, 16, COLS), BF),
            pltpu.VMEM((MATES + 2, 2, 4, 16, COLS), BF),
            pltpu.VMEM((MATES + 2, 2 * EDGE, COLS), BF),
            pltpu.VMEM((2, 32, COLS), BF),
            pltpu.VMEM((2, 32, COLS), BF),
            pltpu.VMEM((2, 32, COLS), F32),
            pltpu.VMEM((5 * 2 * WINDOW * 8, COLS), F32),
            pltpu.VMEM((5 * 128, COLS), F32),
            pltpu.VMEM((128, COLS), F32),
            pltpu.SemaphoreType.DMA,
            pltpu.SemaphoreType.DMA((2,)),
            pltpu.SemaphoreType.DMA((2,)),
            pltpu.SemaphoreType.DMA((5,)),
            pltpu.SemaphoreType.DMA((MATES + 2,)),
            pltpu.SemaphoreType.DMA((4,)),
            pltpu.SemaphoreType.DMA((MATES,)),
            pltpu.SemaphoreType.DMA((MATES + 2,)),
        ],
        compiler_params=pltpu.CompilerParams(
            collective_id=0, has_side_effects=True, vmem_limit_bytes=24 << 20
        ),
        name="coherence",
    )(pltpu.with_memory_space_constraint(images, pltpu.HBM))


def solution(mesh):
    return jax.shard_map(
        per_device,
        mesh=mesh,
        in_specs=(P(None, ("pi", "pj"), "pix", None),),
        out_specs=P("pi", "pj", "pix", None),
        check_vma=False,
    )
```

```python
import jax
import jax.numpy as jnp
from jax import lax
from jax.experimental import pallas as pl
from jax.experimental.pallas import tpu as pltpu
from jax.sharding import PartitionSpec as P

BF = jnp.bfloat16
F32 = jnp.float32
MESH = pl.DeviceIdType.MESH
STRIP = 16
INNER = 10
COLS = 128
MATES = 8
EDGE = 24


def table_row(group, part, row):
    return ((group * 2 + part) * STRIP + row) * 8


def margin_row(group, part, row):
    return ((group * 2 + part) * 6 + row) * 8


def inner_sums(x):
    pairs = {j: x[j] + x[j + 1] for j in range(1, 15, 2)}
    full = []
    for s in range(0, 10, 2):
        middle = pairs[s + 1] + pairs[s + 3] + pairs[s + 5]
        full.append(x[s] + middle)
        full.append(middle + x[s + 7])
    first = (x[0] + pairs[1]) + x[3]
    second = first + x[4]
    last = (x[12] + pairs[13]) + x[15]
    before = x[11] + last
    return full, [first, second, second + x[5], x[10] + before, before, last]


def outer_sums(inside, x):
    above, below = x[1] + x[2], x[3] + x[4]
    return [
        inside[0] + (x[0] + above), inside[1] + above, inside[2] + x[2],
        inside[3] + x[3], inside[4] + below, inside[5] + (below + x[5]),
    ]


def sum_columns(rows, band):
    x = jnp.concatenate(rows, axis=0)
    high = x.astype(BF)
    low = (x - high.astype(F32)).astype(BF)
    return jnp.dot(jnp.concatenate([high, low], axis=1), band, preferred_element_type=F32)


def band_matrix():
    r = lax.broadcasted_iota(jnp.int32, (COLS, COLS), 0)
    c = lax.broadcasted_iota(jnp.int32, (COLS, COLS), 1)
    band = jnp.where(jnp.abs(r - c) <= 3, 1.0, 0.0).astype(BF)
    return jnp.concatenate([band, band], axis=0)


def spread_image(block, table, group, half):
    for part in range(2):
        for p in range(4):
            rows = block[part, p].astype(F32)
            for j in range(2):
                start = table_row(group, part, 8 * j) + half * 4 + p
                table[pl.ds(start, 8, stride=8), :] = rows[8 * j : 8 * j + 8]


def spread_halo(halo, margin, group, half):
    rows = halo[...].astype(F32)
    for edge in range(2):
        for part in range(2):
            for k in range(3):
                start = margin_row(group, part, 3 * edge + k) + half * 4
                first = EDGE * edge + (part * 3 + k) * 4
                margin[pl.ds(start, 4), :] = rows[first : first + 4]


def powers(load, rows):
    out = []
    for row in rows:
        a, b = load(0, row), load(1, row)
        out.append(a * a + b * b)
    return out


def products(first, second, rows):
    real, imag = [], []
    for row in rows:
        a = jnp.broadcast_to(first(0, row), (8, COLS))
        b = jnp.broadcast_to(first(1, row), (8, COLS))
        c, d = second(0, row), second(1, row)
        real.append(a * c + b * d)
        imag.append(b * c - a * d)
    return real, imag


def magnitude(x, y, first, second):
    q = x * x + y * y
    return (q * lax.rsqrt(jnp.maximum(q, 1e-36))) * (jnp.broadcast_to(first, (8, COLS)) * second)


def inner_scale(table, scale, group, band):
    full, _ = inner_sums(powers(lambda part, row: table[pl.ds(table_row(group, part, row), 8), :], range(STRIP)))
    scale[pl.ds(group * 8 * INNER, 8 * INNER), :] = lax.rsqrt(sum_columns(full, band))


def outer_scale(table, margin, scale, group, band):
    x = powers(lambda part, row: table[pl.ds(table_row(group, part, row), 8), :], range(STRIP))
    y = powers(lambda part, row: margin[pl.ds(margin_row(group, part, row), 8), :], range(6))
    scale[pl.ds(group * 8 * 6, 8 * 6), :] = lax.rsqrt(sum_columns(outer_sums(inner_sums(x)[1], y), band))


def inner_rows(group, s, second, table, scale, stage, inside, band):
    m = group * 8 + s
    real, imag = products(
        lambda part, row: table[pl.ds(table_row(group, part, row) + s, 1), :],
        lambda part, row: table[pl.ds(table_row(second, part, row), 8), :],
        range(STRIP),
    )
    real, real_inside = inner_sums(real)
    imag, imag_inside = inner_sums(imag)
    for i, value in enumerate(real_inside + imag_inside):
        inside[pl.ds((m * 12 + i) * 8, 8), :] = value
    w = sum_columns(real + imag, band)
    for r in range(INNER):
        value = magnitude(
            w[r * 8 : r * 8 + 8],
            w[(INNER + r) * 8 : (INNER + r) * 8 + 8],
            scale[pl.ds((group * INNER + r) * 8 + s, 1), :],
            scale[pl.ds((second * INNER + r) * 8, 8), :],
        )
        stage[pl.ds(m * 8 * STRIP + 3 + r, 8, stride=STRIP), :] = value


def outer_rows(base, s, second, margin, scale, stage, inside, edge_stage, out, band):
    group, m = base // 8, base + s
    real, imag = products(
        lambda part, row: margin[pl.ds(margin_row(group, part, row) + s, 1), :],
        lambda part, row: margin[pl.ds(margin_row(second, part, row), 8), :],
        range(6),
    )
    kept = [inside[pl.ds((m * 12 + i) * 8, 8), :] for i in range(12)]
    w = sum_columns(outer_sums(kept[:6], real) + outer_sums(kept[6:], imag), band)
    for i, r in enumerate((0, 1, 2, 5, 6, 7)):
        value = magnitude(
            w[i * 8 : i * 8 + 8],
            w[(6 + i) * 8 : (6 + i) * 8 + 8],
            scale[pl.ds((group * 6 + i) * 8 + s, 1), :],
            scale[pl.ds((second * 6 + i) * 8, 8), :],
        )
        edge_stage[pl.ds(r, 8, stride=8), :] = value
    row = lax.broadcasted_iota(jnp.int32, (8, COLS), 0)
    for n in range(8):
        edge = edge_stage[pl.ds(n * 8, 8), :]
        start = (m * 8 + n) * STRIP
        top = jnp.where(row < 3, edge, stage[pl.ds(start, 8), :])
        bottom = jnp.where(row > 4, edge, stage[pl.ds(start + 8, 8), :])
        out[m, n] = jnp.concatenate([top, bottom], axis=0).astype(BF)


def gather_kernel(images, table, halos, scale, stage, inside, own, blocks, edges, from_strips, edge_rows,
                  ready, own_sem, pix_send, pix_recv, block_send, block_recv, pass_send, halo_send, halo_recv):
    pi, pj, pix = lax.axis_index("pi"), lax.axis_index("pj"), lax.axis_index("pix")
    last = lax.axis_size("pix") - 1
    chip, core = pj // 2, lax.rem(pj, 2)
    far = (pj // 4) != pi
    not_first, not_last = pix > 0, pix < last

    def mate(chips, cores=0):
        return {"pj": 2 * lax.rem(chip + chips, 4) + lax.rem(core + cores, 2)}

    mates = [mate(3, 0), mate(3, 1), mate(2, 0), mate(2, 1), mate(1, 0), mate(1, 1), mate(0, 1)]
    far_target = {"pi": 1 - pi, "pj": 4 * pi + chip}

    fetch = pltpu.make_async_copy(images, own, own_sem)
    fetch.start()
    barrier = pltpu.get_barrier_semaphore()
    upper = pi == 1
    far_sources = [{"pi": 1 - pi, "pj": 2 * lax.rem(pj, 4) + c} for c in range(2)]

    def greet(device):
        pl.semaphore_signal(barrier, inc=1, device_id=device, device_id_type=MESH)

    @pl.when(jnp.logical_not(upper))
    def _():
        greet(far_target)

        @pl.when(far)
        def _():
            for device in far_sources:
                greet(device)

    for device in mates:
        greet(device)

    @pl.when(not_first)
    def _():
        greet({"pix": pix - 1})

    @pl.when(not_last)
    def _():
        greet({"pix": pix + 1})

    band = band_matrix()
    fetch.wait()
    def prepare():
        spread_image(own, table, chip, core)
        edge_rows[...] = jnp.zeros_like(edge_rows)
        for edge in range(2):
            for part in range(2):
                for k in range(3):
                    start = table_row(chip, part, (0 if edge == 0 else 13) + k) + core * 4
                    edge_rows[edge, pl.ds((part * 3 + k) * 4, 4), :] = table[pl.ds(start, 4), :]
        edges[...] = edge_rows[...].astype(BF)

    @pl.when(jnp.logical_not(upper))
    def _():
        prepare()

    strips = not_first.astype(jnp.int32) + not_last.astype(jnp.int32)
    from_lower = jnp.where(upper, jnp.where(far, 3, 1), 0)
    pl.semaphore_wait(barrier, MATES - 1 + strips + from_lower)

    @pl.when(jnp.logical_and(upper, far))
    def _():
        for device in far_sources:
            pl.semaphore_signal(ready, inc=1, device_id=device, device_id_type=MESH)


    def to_strip(edge, strip):
        return pltpu.make_async_remote_copy(
            src_ref=edges.at[edge], dst_ref=from_strips.at[1 - edge], send_sem=pix_send.at[edge],
            recv_sem=pix_recv.at[1 - edge], device_id={"pix": strip}, device_id_type=MESH)

    def send(source, place, slot, send_sem, recv_sem, device):
        copy = pltpu.make_async_remote_copy(
            src_ref=source, dst_ref=place.at[slot], send_sem=send_sem,
            recv_sem=recv_sem.at[slot], device_id=device, device_id_type=MESH)
        copy.start()
        return copy

    def to_far():
        return pltpu.make_async_remote_copy(
            src_ref=own, dst_ref=blocks.at[MATES + core], send_sem=block_send.at[0],
            recv_sem=block_recv.at[MATES + core], device_id=far_target, device_id_type=MESH)

    @pl.when(upper)
    def _():
        to_far().start()

    sent = [to_far()]
    for i, device in enumerate((mate(3), mate(2), mate(1), mate(0, 1))):
        sent.append(send(own, blocks, pj, block_send.at[1 + i], block_recv, device))

    @pl.when(upper)
    def _():
        prepare()

    @pl.when(not_first)
    def _():
        to_strip(0, pix - 1).start()

    @pl.when(not_last)
    def _():
        to_strip(1, pix + 1).start()

    @pl.when(jnp.logical_not(upper))
    def _():
        pl.semaphore_wait(ready, 1)
        to_far().start()

    @pl.when(not_first)
    def _():
        to_strip(1, pix - 1).wait_recv()

    @pl.when(not_last)
    def _():
        to_strip(0, pix + 1).wait_recv()

    @pl.when(jnp.logical_not(not_first))
    def _():
        from_strips[0] = jnp.zeros((32, COLS), BF)

    @pl.when(jnp.logical_not(not_last))
    def _():
        from_strips[1] = jnp.zeros((32, COLS), BF)

    both = jnp.concatenate([from_strips[edge].astype(F32)[:EDGE] for edge in range(2)], axis=0)
    halos[pj] = both.astype(BF)
    sent.append(send(halos.at[pj], halos, MATES + core, halo_send.at[0], halo_recv, far_target))
    for i, device in enumerate(mates):
        sent.append(send(halos.at[pj], halos, pj, halo_send.at[1 + i], halo_recv, device))

    def arrived(slot, place, sem):
        pltpu.make_async_remote_copy(
            src_ref=place.at[slot], dst_ref=place.at[slot], send_sem=sem.at[slot], recv_sem=sem.at[slot],
            device_id=mate(0, 1), device_id_type=MESH).wait_recv()

    for i in range(1, 4):
        slot = 2 * lax.rem(chip + i, 4) + core
        arrived(slot, blocks, block_recv)
        sent.append(send(blocks.at[slot], blocks, slot, pass_send.at[i], block_recv, mate(0, 1)))

    def take(group):
        def one(half, _):
            slot = group * 2 + half

            @pl.when(slot != pj)
            def _():
                @pl.when(jnp.logical_or(half != core, group == MATES // 2))
                def _():
                    arrived(slot, blocks, block_recv)

                spread_image(blocks.at[slot], table, group, half)

            return 0

        lax.fori_loop(0, 2, one, 0)
        inner_scale(table, scale, group, band)

    second = jnp.where(far, MATES // 2, lax.rem(pj, 4))

    @pl.when(far)
    def _():
        def early(i, _):
            take(lax.rem(chip + i, 4))
            return 0

        lax.fori_loop(0, 4, early, 0)

    take(second)

    def step(i, _):
        group = lax.rem(chip + i, 4)

        @pl.when(jnp.logical_not(jnp.logical_or(far, group == second)))
        def _():
            take(group)

        for s in range(8):
            inner_rows(group, s, second, table, scale, stage, inside, band)

        return 0

    lax.fori_loop(0, 4, step, 0)

    def halo_in(slot, _):
        @pl.when(slot != pj)
        def _():
            arrived(slot, halos, halo_recv)

        return 0

    lax.fori_loop(0, jnp.where(far, MATES + 2, MATES), halo_in, 0)
    for copy in sent:
        copy.wait_send()

    @pl.when(not_first)
    def _():
        to_strip(0, pix - 1).wait_send()

    @pl.when(not_last)
    def _():
        to_strip(1, pix + 1).wait_send()


def edge_kernel(table, halos, inner, stage, inside, result, margin, scale, edge_stage, out, out_sem):
    pi, pj = lax.axis_index("pi"), lax.axis_index("pj")
    far = (pj // 4) != pi
    second = jnp.where(far, MATES // 2, lax.rem(pj, 4))
    band = band_matrix()

    def take(group, _):
        for half in range(2):
            spread_halo(halos.at[group * 2 + half], margin, group, half)
        outer_scale(table, margin, scale, group, band)
        return 0

    for g in range(4):
        take(g, 0)

    @pl.when(far)
    def _():
        take(4, 0)

    def write(group):
        return pltpu.make_async_copy(
            out.at[pl.ds(group * 8, 8)], result.at[pl.ds(group * 8, 8)], out_sem.at[group])

    def step(group, _):
        for s in range(8):
            outer_rows(group * 8, s, second, margin, scale, stage, inside, edge_stage.at[group * 8 + s], out, band)
        write(group).start()
        return 0

    for g in range(4):
        step(g, 0)
    for group in range(4):
        write(group).wait()


def second_call(*kept):
    on_chip = pl.BlockSpec(memory_space=pltpu.VMEM)
    return pl.pallas_call(
        edge_kernel,
        out_shape=jax.ShapeDtypeStruct((32, 8, STRIP, COLS), BF),
        in_specs=[on_chip] * 5,
        out_specs=pl.BlockSpec(memory_space=pltpu.HBM),
        scratch_shapes=[
            pltpu.VMEM((5 * 2 * 6 * 8, COLS), F32),
            pltpu.VMEM((5 * 6 * 8, COLS), F32),
            pltpu.VMEM((32, 64, COLS), F32),
            pltpu.VMEM((32, 8, STRIP, COLS), BF),
            pltpu.SemaphoreType.DMA((4,)),
        ],
        compiler_params=pltpu.CompilerParams(vmem_limit_bytes=16 << 20),
        name="coherence_edges",
    )(*kept)


def per_device(images):
    on_chip = pl.BlockSpec(memory_space=pltpu.VMEM)
    kept = pl.pallas_call(
        gather_kernel,
        out_shape=(
            pltpu.VMEM((5 * 2 * STRIP * 8, COLS), F32),
            pltpu.VMEM((MATES + 2, 2 * EDGE, COLS), BF),
            pltpu.VMEM((5 * INNER * 8, COLS), F32),
            pltpu.VMEM((32 * 8 * STRIP, COLS), F32),
            pltpu.VMEM((32 * 12 * 8, COLS), F32),
        ),
        in_specs=[pl.BlockSpec(memory_space=pltpu.HBM)],
        out_specs=(on_chip,) * 5,
        scratch_shapes=[
            pltpu.VMEM((2, 4, 16, COLS), BF),
            pltpu.VMEM((MATES + 2, 2, 4, 16, COLS), BF),
            pltpu.VMEM((2, 32, COLS), BF),
            pltpu.VMEM((2, 32, COLS), BF),
            pltpu.VMEM((2, 32, COLS), F32),
            pltpu.SemaphoreType.REGULAR,
            pltpu.SemaphoreType.DMA,
            pltpu.SemaphoreType.DMA((2,)),
            pltpu.SemaphoreType.DMA((2,)),
            pltpu.SemaphoreType.DMA((5,)),
            pltpu.SemaphoreType.DMA((MATES + 2,)),
            pltpu.SemaphoreType.DMA((4,)),
            pltpu.SemaphoreType.DMA((MATES,)),
            pltpu.SemaphoreType.DMA((MATES + 2,)),
        ],
        compiler_params=pltpu.CompilerParams(
            collective_id=0, has_side_effects=True, vmem_limit_bytes=16 << 20
        ),
        name="coherence_inner",
    )(pltpu.with_memory_space_constraint(images, pltpu.HBM))
    return second_call(*kept)


def solution(mesh):
    return jax.shard_map(
        per_device,
        mesh=mesh,
        in_specs=(P(None, ("pi", "pj"), "pix", None),),
        out_specs=P("pi", "pj", "pix", None),
        check_vma=False,
    )
```

```python
import jax
import jax.numpy as jnp
from jax import lax
from jax.experimental import pallas as pl
from jax.experimental.pallas import tpu as pltpu
from jax.sharding import PartitionSpec as P

BF = jnp.bfloat16
F32 = jnp.float32
MESH = pl.DeviceIdType.MESH
STRIP = 16
INNER = 10
COLS = 128
MATES = 8
EDGE = 24


def table_row(group, part, row):
    return ((group * 2 + part) * STRIP + row) * 8


def margin_row(group, part, row):
    return ((group * 2 + part) * 6 + row) * 8


def inner_sums(x):
    pairs = {j: x[j] + x[j + 1] for j in range(1, 15, 2)}
    full = []
    for s in range(0, 10, 2):
        middle = pairs[s + 1] + pairs[s + 3] + pairs[s + 5]
        full.append(x[s] + middle)
        full.append(middle + x[s + 7])
    first = (x[0] + pairs[1]) + x[3]
    second = first + x[4]
    last = (x[12] + pairs[13]) + x[15]
    before = x[11] + last
    return full, [first, second, second + x[5], x[10] + before, before, last]


def outer_sums(inside, x):
    above, below = x[1] + x[2], x[3] + x[4]
    return [
        inside[0] + (x[0] + above), inside[1] + above, inside[2] + x[2],
        inside[3] + x[3], inside[4] + below, inside[5] + (below + x[5]),
    ]


def sum_columns(rows, band):
    x = jnp.concatenate(rows, axis=0)
    high = x.astype(BF)
    low = (x - high.astype(F32)).astype(BF)
    return jnp.dot(jnp.concatenate([high, low], axis=1), band, preferred_element_type=F32)


def band_matrix():
    r = lax.broadcasted_iota(jnp.int32, (COLS, COLS), 0)
    c = lax.broadcasted_iota(jnp.int32, (COLS, COLS), 1)
    band = jnp.where(jnp.abs(r - c) <= 3, 1.0, 0.0).astype(BF)
    return jnp.concatenate([band, band], axis=0)


def spread_image(block, table, group, half):
    for part in range(2):
        for p in range(4):
            rows = block[part, p].astype(F32)
            for j in range(2):
                start = table_row(group, part, 8 * j) + half * 4 + p
                table[pl.ds(start, 8, stride=8), :] = rows[8 * j : 8 * j + 8]


def spread_halo(halo, margin, group, half):
    rows = halo[...].astype(F32)
    for edge in range(2):
        for part in range(2):
            for k in range(3):
                start = margin_row(group, part, 3 * edge + k) + half * 4
                first = EDGE * edge + (part * 3 + k) * 4
                margin[pl.ds(start, 4), :] = rows[first : first + 4]


def powers(load, rows):
    out = []
    for row in rows:
        a, b = load(0, row), load(1, row)
        out.append(a * a + b * b)
    return out


def products(first, second, rows):
    real, imag = [], []
    for row in rows:
        a = jnp.broadcast_to(first(0, row), (8, COLS))
        b = jnp.broadcast_to(first(1, row), (8, COLS))
        c, d = second(0, row), second(1, row)
        real.append(a * c + b * d)
        imag.append(b * c - a * d)
    return real, imag


def magnitude(x, y, first, second):
    q = x * x + y * y
    return (q * lax.rsqrt(jnp.maximum(q, 1e-36))) * (jnp.broadcast_to(first, (8, COLS)) * second)


def inner_scale(table, scale, group, band):
    full, _ = inner_sums(powers(lambda part, row: table[pl.ds(table_row(group, part, row), 8), :], range(STRIP)))
    scale[pl.ds(group * 8 * INNER, 8 * INNER), :] = lax.rsqrt(sum_columns(full, band))


def outer_scale(table, margin, scale, group, band):
    x = powers(lambda part, row: table[pl.ds(table_row(group, part, row), 8), :], range(STRIP))
    y = powers(lambda part, row: margin[pl.ds(margin_row(group, part, row), 8), :], range(6))
    scale[pl.ds(group * 8 * 6, 8 * 6), :] = lax.rsqrt(sum_columns(outer_sums(inner_sums(x)[1], y), band))


def inner_rows(group, s, second, table, scale, stage, inside, band):
    m = group * 8 + s
    real, imag = products(
        lambda part, row: table[pl.ds(table_row(group, part, row) + s, 1), :],
        lambda part, row: table[pl.ds(table_row(second, part, row), 8), :],
        range(STRIP),
    )
    real, real_inside = inner_sums(real)
    imag, imag_inside = inner_sums(imag)
    for i, value in enumerate(real_inside + imag_inside):
        inside[pl.ds((m * 12 + i) * 8, 8), :] = value
    w = sum_columns(real + imag, band)
    for r in range(INNER):
        value = magnitude(
            w[r * 8 : r * 8 + 8],
            w[(INNER + r) * 8 : (INNER + r) * 8 + 8],
            scale[pl.ds((group * INNER + r) * 8 + s, 1), :],
            scale[pl.ds((second * INNER + r) * 8, 8), :],
        )
        stage[pl.ds(m * 8 * STRIP + 3 + r, 8, stride=STRIP), :] = value


def outer_rows(base, s, second, margin, scale, stage, inside, edge_stage, out, band):
    group, m = base // 8, base + s
    real, imag = products(
        lambda part, row: margin[pl.ds(margin_row(group, part, row) + s, 1), :],
        lambda part, row: margin[pl.ds(margin_row(second, part, row), 8), :],
        range(6),
    )
    kept = [inside[pl.ds((m * 12 + i) * 8, 8), :] for i in range(12)]
    w = sum_columns(outer_sums(kept[:6], real) + outer_sums(kept[6:], imag), band)
    for i, r in enumerate((0, 1, 2, 5, 6, 7)):
        value = magnitude(
            w[i * 8 : i * 8 + 8],
            w[(6 + i) * 8 : (6 + i) * 8 + 8],
            scale[pl.ds((group * 6 + i) * 8 + s, 1), :],
            scale[pl.ds((second * 6 + i) * 8, 8), :],
        )
        edge_stage[pl.ds(r, 8, stride=8), :] = value
    row = lax.broadcasted_iota(jnp.int32, (8, COLS), 0)
    for n in range(8):
        edge = edge_stage[pl.ds(n * 8, 8), :]
        start = (m * 8 + n) * STRIP
        top = jnp.where(row < 3, edge, stage[pl.ds(start, 8), :])
        bottom = jnp.where(row > 4, edge, stage[pl.ds(start + 8, 8), :])
        out[m, n] = jnp.concatenate([top, bottom], axis=0).astype(BF)


def gather_kernel(images, table, halos, scale, stage, inside, own, blocks, edges, from_strips, edge_rows,
                  ready, late, own_sem, pix_send, pix_recv, block_send, block_recv, pass_send, halo_send, halo_recv,
                  hand_send, pass_halo):
    pi, pj, pix = lax.axis_index("pi"), lax.axis_index("pj"), lax.axis_index("pix")
    last = lax.axis_size("pix") - 1
    chip, core = pj // 2, lax.rem(pj, 2)
    far = (pj // 4) != pi
    upper = pi == 1
    lower = jnp.logical_not(upper)
    not_first, not_last = pix > 0, pix < last

    def both(a, b):
        return jnp.logical_and(a, b)

    first_column = both(lower, pix == 0)
    corner = both(first_column, pj == 0)
    corner_mate = both(first_column, pj != 0)
    sibling = both(first_column, pj == 1)
    corner_strip = both(lower, both(pix == 1, pj == 0))
    corner_far = both(upper, both(pix == 0, pj == 0))

    def number(condition):
        return condition.astype(jnp.int32)

    def mate(chips, cores=0):
        return {"pj": 2 * lax.rem(chip + chips, 4) + lax.rem(core + cores, 2)}

    mates = [mate(3, 0), mate(3, 1), mate(2, 0), mate(2, 1), mate(1, 0), mate(1, 1), mate(0, 1)]
    far_target = {"pi": 1 - pi, "pj": 4 * pi + chip}
    far_sources = [{"pi": 1 - pi, "pj": 2 * lax.rem(pj, 4) + c} for c in range(2)]

    fetch = pltpu.make_async_copy(images, own, own_sem)
    fetch.start()
    barrier = pltpu.get_barrier_semaphore()

    def greet(device):
        pl.semaphore_signal(barrier, inc=1, device_id=device, device_id_type=MESH)

    @pl.when(jnp.logical_not(corner))
    def _():
        @pl.when(lower)
        def _():
            greet(far_target)

            @pl.when(far)
            def _():
                for device in far_sources:
                    greet(device)

        for device in mates:
            greet(device)

        @pl.when(corner_far)
        def _():
            greet(far_sources[0])

        @pl.when(not_first)
        def _():
            greet({"pix": pix - 1})

        @pl.when(not_last)
        def _():
            greet({"pix": pix + 1})

    band = band_matrix()

    def prepare():
        spread_image(own, table, chip, core)
        edge_rows[...] = jnp.zeros_like(edge_rows)
        for edge in range(2):
            for part in range(2):
                for k in range(3):
                    start = table_row(chip, part, (0 if edge == 0 else 13) + k) + core * 4
                    edge_rows[edge, pl.ds((part * 3 + k) * 4, 4), :] = table[pl.ds(start, 4), :]
        edges[...] = edge_rows[...].astype(BF)

    @pl.when(lower)
    def _():
        fetch.wait()
        prepare()

    from_lower = jnp.where(upper, jnp.where(far, 3, 1), 0)
    greetings = MATES - 1 + number(not_first) + number(not_last) + from_lower
    pl.semaphore_wait(
        barrier, greetings + number(corner) - number(corner_mate) - number(corner_strip) - number(corner_far))

    @pl.when(both(upper, far))
    def _():
        @pl.when(jnp.logical_not(corner_far))
        def _():
            pl.semaphore_signal(ready, inc=1, device_id=far_sources[0], device_id_type=MESH)

        pl.semaphore_signal(ready, inc=1, device_id=far_sources[1], device_id_type=MESH)

    @pl.when(corner)
    def _():
        for device in ({"pj": 1}, {"pix": 1}):
            pl.semaphore_signal(late, inc=1, device_id=device, device_id_type=MESH)

    def to_strip(edge, strip):
        return pltpu.make_async_remote_copy(
            src_ref=edges.at[edge], dst_ref=from_strips.at[1 - edge], send_sem=pix_send.at[edge],
            recv_sem=pix_recv.at[1 - edge], device_id={"pix": strip}, device_id_type=MESH)

    def sending(source, place, slot, send_sem, recv_sem, device):
        return pltpu.make_async_remote_copy(
            src_ref=source, dst_ref=place.at[slot], send_sem=send_sem,
            recv_sem=recv_sem.at[slot], device_id=device, device_id_type=MESH)

    sent = []

    def is_corner(device):
        return both(corner_mate, device["pj"] == 0)

    def send(copy, condition):
        @pl.when(condition)
        def _():
            copy.start()

    def send_to_mates(source, place, send_sem, recv_sem):
        for i, device in enumerate((mate(3), mate(2), mate(1), mate(0, 1))):
            target = jnp.where(both(is_corner(device), pj != 1), 1, device["pj"])
            copy = sending(source, place, pj, send_sem.at[1 + i], recv_sem, {"pj": target})
            send(copy, jnp.logical_not(both(sibling, target == 0)))
            sent.append(copy)

    to_far = sending(own, blocks, MATES + core, block_send.at[0], block_recv, far_target)
    sent.append(to_far)

    @pl.when(upper)
    def _():
        fetch.wait()

    @pl.when(jnp.logical_or(upper, corner))
    def _():
        to_far.start()

    send_to_mates(own, blocks, block_send, block_recv)

    @pl.when(upper)
    def _():
        prepare()

    @pl.when(both(not_first, jnp.logical_not(corner_strip)))
    def _():
        to_strip(0, pix - 1).start()

    @pl.when(not_last)
    def _():
        to_strip(1, pix + 1).start()

    @pl.when(both(lower, jnp.logical_not(corner)))
    def _():
        pl.semaphore_wait(ready, 1)
        to_far.start()

    def arrived(slot, place, sem):
        sending(place.at[slot], place, slot, sem.at[slot], sem, mate(0, 1)).wait_recv()

    @pl.when(not_first)
    def _():
        to_strip(1, pix - 1).wait_recv()

    @pl.when(not_last)
    def _():
        to_strip(0, pix + 1).wait_recv()

    @pl.when(jnp.logical_not(not_first))
    def _():
        from_strips[0] = jnp.zeros((32, COLS), BF)

    @pl.when(jnp.logical_not(not_last))
    def _():
        from_strips[1] = jnp.zeros((32, COLS), BF)

    rows = jnp.concatenate([from_strips[edge].astype(F32)[:EDGE] for edge in range(2)], axis=0)
    halos[pj] = rows.astype(BF)
    far_halo = sending(halos.at[pj], halos, MATES + core, halo_send.at[0], halo_recv, far_target)
    far_halo.start()
    sent.append(far_halo)
    send_to_mates(halos.at[pj], halos, halo_send, halo_recv)

    def hand_over(i, place, send_sem, recv_sem):
        slot = 2 * lax.rem(chip + i, 4) + core
        return slot, sending(place.at[slot], place, slot, send_sem.at[i], recv_sem, mate(0, 1))

    def hand_all_over(place, send_sem, recv_sem):
        for i in range(1, 4):
            slot, copy = hand_over(i, place, send_sem, recv_sem)

            @pl.when(jnp.logical_not(jnp.logical_or(corner, both(corner_mate, slot == 0))))
            def _():
                arrived(slot, place, recv_sem)
                send(copy, jnp.logical_not(sibling))

    def hand_corner_over(place, send_sem, recv_sem):
        for i in range(1, 4):
            slot, copy = hand_over(i, place, send_sem, recv_sem)

            @pl.when(both(corner_mate, slot == 0))
            def _():
                arrived(slot, place, recv_sem)
                copy.start()

    hand_all_over(blocks, pass_send, block_recv)

    @pl.when(corner_strip)
    def _():
        pl.semaphore_wait(late, 1)
        to_strip(0, pix - 1).start()

    def to_corner(slot, place, sem, send_sem):
        return sending(place.at[slot], place, slot, send_sem, sem, {"pj": 0})

    def serve_corner():
        pl.semaphore_wait(late, 1)
        sending(own, blocks, pj, block_send.at[4], block_recv, {"pj": 0}).start()
        sending(halos.at[pj], halos, pj, halo_send.at[4], halo_recv, {"pj": 0}).start()
        for i in range(1, 4):
            hand_over(i, blocks, pass_send, block_recv)[1].start()
            to_corner(2 * i, blocks, block_recv, pass_send.at[3 + i]).start()

    def take(group):
        def one(half, _):
            slot = group * 2 + half

            @pl.when(slot != pj)
            def _():
                @pl.when(jnp.logical_or(corner, jnp.logical_or(half != core, group == MATES // 2)))
                def _():
                    arrived(slot, blocks, block_recv)

                spread_image(blocks.at[slot], table, group, half)

            return 0

        lax.fori_loop(0, 2, one, 0)
        inner_scale(table, scale, group, band)

    def group_at(i):
        ahead = lax.rem(chip + i + number(both(corner_mate, chip == 0)), 4)
        return jnp.where(chip < 2, ahead, jnp.where(both(chip == 2, i < 2), 2 + i, 3 - i))

    second = jnp.where(far, MATES // 2, lax.rem(pj, 4))

    eager = jnp.logical_or(far, sibling)

    @pl.when(eager)
    def _():
        def early(i, _):
            take(group_at(i))
            return 0

        lax.fori_loop(0, 4 - number(corner_mate), early, 0)

    @pl.when(sibling)
    def _():
        serve_corner()


    @pl.when(jnp.logical_not(sibling))
    def _():
        take(second)

    def step(i, _):
        group = group_at(i)

        @pl.when(i == 2)
        def _():
            hand_all_over(halos, pass_halo, halo_recv)

        @pl.when(i == 3)
        def _():
            hand_corner_over(blocks, pass_send, block_recv)

        @pl.when(jnp.logical_or(both(jnp.logical_not(eager), group != second), both(eager, both(corner_mate, i == 3))))
        def _():
            take(group)

        for s in range(8):
            inner_rows(group, s, second, table, scale, stage, inside, band)

        return 0

    lax.fori_loop(0, 4, step, 0)

    def halo_in(slot, _):
        @pl.when(slot != pj)
        def _():
            @pl.when(jnp.logical_or(corner, jnp.logical_or(lax.rem(slot, 2) != core, slot >= MATES)))
            def _():
                arrived(slot, halos, halo_recv)

            @pl.when(both(sibling, slot > 1))
            def _():
                to_corner(slot, halos, halo_recv, hand_send.at[slot]).start()

        return 0

    lax.fori_loop(0, jnp.where(far, MATES + 2, MATES), halo_in, 0)
    hand_corner_over(halos, pass_halo, halo_recv)
    for copy in sent:
        copy.wait_send()

    @pl.when(jnp.logical_not(corner))
    def _():
        for i in range(1, 4):
            hand_over(i, blocks, pass_send, block_recv)[1].wait_send()

    @pl.when(jnp.logical_not(jnp.logical_or(corner, sibling)))
    def _():
        for i in range(1, 4):
            hand_over(i, halos, pass_halo, halo_recv)[1].wait_send()

    @pl.when(sibling)
    def _():
        for i in range(1, 4):
            to_corner(2 * i, blocks, block_recv, pass_send.at[3 + i]).wait_send()
        for slot in range(2, MATES):
            to_corner(slot, halos, halo_recv, hand_send.at[slot]).wait_send()

    @pl.when(not_first)
    def _():
        to_strip(0, pix - 1).wait_send()

    @pl.when(not_last)
    def _():
        to_strip(1, pix + 1).wait_send()


def edge_kernel(table, halos, inner, stage, inside, result, margin, scale, edge_stage, out, out_sem):
    pi, pj = lax.axis_index("pi"), lax.axis_index("pj")
    far = (pj // 4) != pi
    second = jnp.where(far, MATES // 2, lax.rem(pj, 4))
    band = band_matrix()

    def take(group, _):
        for half in range(2):
            spread_halo(halos.at[group * 2 + half], margin, group, half)
        outer_scale(table, margin, scale, group, band)
        return 0

    for g in range(4):
        take(g, 0)

    @pl.when(far)
    def _():
        take(4, 0)

    def write(group):
        return pltpu.make_async_copy(
            out.at[pl.ds(group * 8, 8)], result.at[pl.ds(group * 8, 8)], out_sem.at[group])

    def step(group, _):
        for s in range(8):
            outer_rows(group * 8, s, second, margin, scale, stage, inside, edge_stage.at[group * 8 + s], out, band)
        write(group).start()
        return 0

    for g in range(4):
        step(g, 0)
    for group in range(4):
        write(group).wait()


def second_call(*kept):
    on_chip = pl.BlockSpec(memory_space=pltpu.VMEM)
    return pl.pallas_call(
        edge_kernel,
        out_shape=jax.ShapeDtypeStruct((32, 8, STRIP, COLS), BF),
        in_specs=[on_chip] * 5,
        out_specs=pl.BlockSpec(memory_space=pltpu.HBM),
        scratch_shapes=[
            pltpu.VMEM((5 * 2 * 6 * 8, COLS), F32),
            pltpu.VMEM((5 * 6 * 8, COLS), F32),
            pltpu.VMEM((32, 64, COLS), F32),
            pltpu.VMEM((32, 8, STRIP, COLS), BF),
            pltpu.SemaphoreType.DMA((4,)),
        ],
        compiler_params=pltpu.CompilerParams(vmem_limit_bytes=16 << 20),
        name="coherence_edges",
    )(*kept)


def per_device(images):
    on_chip = pl.BlockSpec(memory_space=pltpu.VMEM)
    kept = pl.pallas_call(
        gather_kernel,
        out_shape=(
            pltpu.VMEM((5 * 2 * STRIP * 8, COLS), F32),
            pltpu.VMEM((MATES + 2, 2 * EDGE, COLS), BF),
            pltpu.VMEM((5 * INNER * 8, COLS), F32),
            pltpu.VMEM((32 * 8 * STRIP, COLS), F32),
            pltpu.VMEM((32 * 12 * 8, COLS), F32),
        ),
        in_specs=[pl.BlockSpec(memory_space=pltpu.HBM)],
        out_specs=(on_chip,) * 5,
        scratch_shapes=[
            pltpu.VMEM((2, 4, 16, COLS), BF),
            pltpu.VMEM((MATES + 2, 2, 4, 16, COLS), BF),
            pltpu.VMEM((2, 32, COLS), BF),
            pltpu.VMEM((2, 32, COLS), BF),
            pltpu.VMEM((2, 32, COLS), F32),
            pltpu.SemaphoreType.REGULAR,
            pltpu.SemaphoreType.REGULAR,
            pltpu.SemaphoreType.DMA,
            pltpu.SemaphoreType.DMA((2,)),
            pltpu.SemaphoreType.DMA((2,)),
            pltpu.SemaphoreType.DMA((5,)),
            pltpu.SemaphoreType.DMA((MATES + 2,)),
            pltpu.SemaphoreType.DMA((7,)),
            pltpu.SemaphoreType.DMA((5,)),
            pltpu.SemaphoreType.DMA((MATES + 2,)),
            pltpu.SemaphoreType.DMA((MATES,)),
            pltpu.SemaphoreType.DMA((4,)),
        ],
        compiler_params=pltpu.CompilerParams(
            collective_id=0, has_side_effects=True, vmem_limit_bytes=16 << 20
        ),
        name="coherence_inner",
    )(pltpu.with_memory_space_constraint(images, pltpu.HBM))
    return second_call(*kept)


def solution(mesh):
    return jax.shard_map(
        per_device,
        mesh=mesh,
        in_specs=(P(None, ("pi", "pj"), "pix", None),),
        out_specs=P("pi", "pj", "pix", None),
        check_vma=False,
    )
```

```python
import jax
import jax.numpy as jnp
from jax import lax
from jax.experimental import pallas as pl
from jax.experimental.pallas import tpu as pltpu
from jax.sharding import PartitionSpec as P

BF = jnp.bfloat16
F32 = jnp.float32
MESH = pl.DeviceIdType.MESH
STRIP = 16
INNER = 10
COLS = 128
MATES = 8
EDGE = 24


def table_row(group, part, row):
    return ((group * 2 + part) * STRIP + row) * 8


def margin_row(group, part, row):
    return ((group * 2 + part) * 6 + row) * 8


def inner_sums(x):
    pairs = {j: x[j] + x[j + 1] for j in range(1, 15, 2)}
    full = []
    for s in range(0, 10, 2):
        middle = pairs[s + 1] + pairs[s + 3] + pairs[s + 5]
        full.append(x[s] + middle)
        full.append(middle + x[s + 7])
    first = (x[0] + pairs[1]) + x[3]
    second = first + x[4]
    last = (x[12] + pairs[13]) + x[15]
    before = x[11] + last
    return full, [first, second, second + x[5], x[10] + before, before, last]


def outer_sums(inside, x):
    above, below = x[1] + x[2], x[3] + x[4]
    return [
        inside[0] + (x[0] + above), inside[1] + above, inside[2] + x[2],
        inside[3] + x[3], inside[4] + below, inside[5] + (below + x[5]),
    ]


def sum_columns(rows, band):
    x = jnp.concatenate(rows, axis=0)
    high = x.astype(BF)
    low = (x - high.astype(F32)).astype(BF)
    return jnp.dot(jnp.concatenate([high, low], axis=1), band, preferred_element_type=F32)


def band_matrix():
    r = lax.broadcasted_iota(jnp.int32, (COLS, COLS), 0)
    c = lax.broadcasted_iota(jnp.int32, (COLS, COLS), 1)
    band = jnp.where(jnp.abs(r - c) <= 3, 1.0, 0.0).astype(BF)
    return jnp.concatenate([band, band], axis=0)


def spread_image(block, table, group, half):
    for part in range(2):
        for p in range(4):
            rows = block[part, p].astype(F32)
            for j in range(2):
                start = table_row(group, part, 8 * j) + half * 4 + p
                table[pl.ds(start, 8, stride=8), :] = rows[8 * j : 8 * j + 8]


def spread_halo(halo, margin, group, half):
    rows = halo[...].astype(F32)
    for edge in range(2):
        for part in range(2):
            for k in range(3):
                start = margin_row(group, part, 3 * edge + k) + half * 4
                first = EDGE * edge + (part * 3 + k) * 4
                margin[pl.ds(start, 4), :] = rows[first : first + 4]


def powers(load, rows):
    out = []
    for row in rows:
        a, b = load(0, row), load(1, row)
        out.append(a * a + b * b)
    return out


def products(first, second, rows):
    real, imag = [], []
    for row in rows:
        a = jnp.broadcast_to(first(0, row), (8, COLS))
        b = jnp.broadcast_to(first(1, row), (8, COLS))
        c, d = second(0, row), second(1, row)
        real.append(a * c + b * d)
        imag.append(b * c - a * d)
    return real, imag


def magnitude(x, y, first, second):
    q = x * x + y * y
    return (q * lax.rsqrt(jnp.maximum(q, 1e-36))) * (jnp.broadcast_to(first, (8, COLS)) * second)


def inner_scale(table, scale, group, band):
    full, _ = inner_sums(powers(lambda part, row: table[pl.ds(table_row(group, part, row), 8), :], range(STRIP)))
    scale[pl.ds(group * 8 * INNER, 8 * INNER), :] = lax.rsqrt(sum_columns(full, band))


def outer_scale(table, margin, scale, group, source, band):
    x = powers(lambda part, row: table[pl.ds(table_row(source, part, row), 8), :], range(STRIP))
    y = powers(lambda part, row: margin[pl.ds(margin_row(group, part, row), 8), :], range(6))
    scale[pl.ds(group * 8 * 6, 8 * 6), :] = lax.rsqrt(sum_columns(outer_sums(inner_sums(x)[1], y), band))


def inner_rows(group, s, second, table, scale, stage, inside, band):
    m = group * 8 + s
    real, imag = products(
        lambda part, row: table[pl.ds(table_row(group, part, row) + s, 1), :],
        lambda part, row: table[pl.ds(table_row(second, part, row), 8), :],
        range(STRIP),
    )
    real, real_inside = inner_sums(real)
    imag, imag_inside = inner_sums(imag)
    for i, value in enumerate(real_inside + imag_inside):
        inside[pl.ds((m * 12 + i) * 8, 8), :] = value
    w = sum_columns(real + imag, band)
    for r in range(INNER):
        value = magnitude(
            w[r * 8 : r * 8 + 8],
            w[(INNER + r) * 8 : (INNER + r) * 8 + 8],
            scale[pl.ds((group * INNER + r) * 8 + s, 1), :],
            scale[pl.ds((second * INNER + r) * 8, 8), :],
        )
        stage[pl.ds(m * 8 * STRIP + 3 + r, 8, stride=STRIP), :] = value


def outer_rows(group, s, margin, scale, stage, inside, edge_stage, out, band):
    m = group * 8 + s
    real, imag = products(
        lambda part, row: margin[pl.ds(margin_row(group, part, row) + s, 1), :],
        lambda part, row: margin[pl.ds(margin_row(4, part, row), 8), :],
        range(6),
    )
    kept = [inside[pl.ds((m * 12 + i) * 8, 8), :] for i in range(12)]
    w = sum_columns(outer_sums(kept[:6], real) + outer_sums(kept[6:], imag), band)
    for i, r in enumerate((0, 1, 2, 5, 6, 7)):
        value = magnitude(
            w[i * 8 : i * 8 + 8],
            w[(6 + i) * 8 : (6 + i) * 8 + 8],
            scale[pl.ds((group * 6 + i) * 8 + s, 1), :],
            scale[pl.ds((4 * 6 + i) * 8, 8), :],
        )
        edge_stage[pl.ds(r, 8, stride=8), :] = value
    row = lax.broadcasted_iota(jnp.int32, (8, COLS), 0)
    for n in range(8):
        edge = edge_stage[pl.ds(n * 8, 8), :]
        start = (m * 8 + n) * STRIP
        top = jnp.where(row < 3, edge, stage[pl.ds(start, 8), :])
        bottom = jnp.where(row > 4, edge, stage[pl.ds(start + 8, 8), :])
        out[m, n] = jnp.concatenate([top, bottom], axis=0).astype(BF)


def gather_kernel(images, table, halos, scale, stage, inside, own, blocks, edges, from_strips, edge_rows,
                  ready, late, next_ready, own_sem, pix_send, pix_recv, block_send, block_recv, pass_send, halo_send, halo_recv,
                  hand_send, pass_halo):
    pi, pj, pix = lax.axis_index("pi"), lax.axis_index("pj"), lax.axis_index("pix")
    last = lax.axis_size("pix") - 1
    chip, core = pj // 2, lax.rem(pj, 2)
    far = (pj // 4) != pi
    upper = pi == 1
    lower = jnp.logical_not(upper)
    not_first, not_last = pix > 0, pix < last

    def both(a, b):
        return jnp.logical_and(a, b)

    first_column = both(lower, pix == 0)
    corner = both(first_column, pj == 0)
    corner_mate = both(first_column, pj != 0)
    sibling = both(first_column, pj == 1)
    corner_strip = both(lower, both(pix == 1, pj == 0))
    corner_far = both(upper, both(pix == 0, pj == 0))

    before_step = both(not_last, both(upper, lax.rem(pix, 4) != 3))
    after_step = both(not_first, both(upper, lax.rem(pix, 4) != 0))

    def number(condition):
        return condition.astype(jnp.int32)

    def mate(chips, cores=0):
        return {"pj": 2 * lax.rem(chip + chips, 4) + lax.rem(core + cores, 2)}

    mates = [mate(3, 0), mate(3, 1), mate(2, 0), mate(2, 1), mate(1, 0), mate(1, 1), mate(0, 1)]
    far_target = {"pi": 1 - pi, "pj": 4 * pi + chip}
    far_sources = [{"pi": 1 - pi, "pj": 2 * lax.rem(pj, 4) + c} for c in range(2)]

    fetch = pltpu.make_async_copy(images, own, own_sem)
    fetch.start()
    barrier = pltpu.get_barrier_semaphore()

    def greet(device):
        pl.semaphore_signal(barrier, inc=1, device_id=device, device_id_type=MESH)

    @pl.when(jnp.logical_not(corner))
    def _():
        @pl.when(lower)
        def _():
            greet(far_target)

            @pl.when(far)
            def _():
                for device in far_sources:
                    greet(device)

        for device in mates:
            greet(device)

        @pl.when(corner_far)
        def _():
            greet(far_sources[0])

        @pl.when(both(not_first, jnp.logical_not(after_step)))
        def _():
            greet({"pix": pix - 1})

        @pl.when(not_last)
        def _():
            greet({"pix": pix + 1})

    band = band_matrix()

    def prepare():
        spread_image(own, table, chip, core)
        edge_rows[...] = jnp.zeros_like(edge_rows)
        for edge in range(2):
            for part in range(2):
                for k in range(3):
                    start = table_row(chip, part, (0 if edge == 0 else 13) + k) + core * 4
                    edge_rows[edge, pl.ds((part * 3 + k) * 4, 4), :] = table[pl.ds(start, 4), :]
        edges[...] = edge_rows[...].astype(BF)

    @pl.when(jnp.logical_not(corner))
    def _():
        fetch.wait()
        prepare()

    from_lower = jnp.where(upper, jnp.where(far, 3, 1), 0)
    greetings = MATES - 1 + number(not_first) + number(not_last) + from_lower
    pl.semaphore_wait(
        barrier, greetings + number(corner) - number(corner_mate) - number(corner_strip) - number(corner_far)
        - number(before_step))

    @pl.when(both(upper, far))
    def _():
        @pl.when(jnp.logical_not(corner_far))
        def _():
            pl.semaphore_signal(ready, inc=1, device_id=far_sources[0], device_id_type=MESH)

        pl.semaphore_signal(ready, inc=1, device_id=far_sources[1], device_id_type=MESH)

    @pl.when(after_step)
    def _():
        pl.semaphore_signal(next_ready, inc=1, device_id={"pix": pix - 1}, device_id_type=MESH)

    @pl.when(corner)
    def _():
        for device in ({"pj": 1}, {"pix": 1}):
            pl.semaphore_signal(late, inc=1, device_id=device, device_id_type=MESH)

    def to_strip(edge, strip):
        return pltpu.make_async_remote_copy(
            src_ref=edges.at[edge], dst_ref=from_strips.at[1 - edge], send_sem=pix_send.at[edge],
            recv_sem=pix_recv.at[1 - edge], device_id={"pix": strip}, device_id_type=MESH)

    def sending(source, place, slot, send_sem, recv_sem, device):
        return pltpu.make_async_remote_copy(
            src_ref=source, dst_ref=place.at[slot], send_sem=send_sem,
            recv_sem=recv_sem.at[slot], device_id=device, device_id_type=MESH)

    sent, sent_by_corner = [], []

    def is_corner(device):
        return both(corner_mate, device["pj"] == 0)

    def send(copy, condition):
        @pl.when(condition)
        def _():
            copy.start()

    def send_to_mates(source, place, send_sem, recv_sem):
        for i, device in enumerate((mate(3), mate(2), mate(1), mate(0, 1))):
            target = jnp.where(both(is_corner(device), pj != 1), 1, device["pj"])
            copy = sending(source, place, pj, send_sem.at[1 + i], recv_sem, {"pj": target})
            send(copy, jnp.logical_not(both(sibling, target == 0)))
            sent.append(copy)
        for i in range(1, 4):
            copy = sending(source, place, pj, send_sem.at[4 + i], recv_sem, mate(i, 1))
            send(copy, corner)
            sent_by_corner.append(copy)

    to_far = sending(own, blocks, MATES + core, block_send.at[0], block_recv, far_target)
    sent.append(to_far)

    @pl.when(corner)
    def _():
        fetch.wait()

    @pl.when(jnp.logical_or(upper, corner))
    def _():
        to_far.start()

    send_to_mates(own, blocks, block_send, block_recv)

    @pl.when(corner)
    def _():
        prepare()

    @pl.when(both(not_first, jnp.logical_not(corner_strip)))
    def _():
        to_strip(0, pix - 1).start()

    @pl.when(both(not_last, jnp.logical_not(before_step)))
    def _():
        to_strip(1, pix + 1).start()

    @pl.when(both(lower, jnp.logical_not(corner)))
    def _():
        pl.semaphore_wait(ready, 1)
        to_far.start()

    @pl.when(before_step)
    def _():
        pl.semaphore_wait(next_ready, 1)
        to_strip(1, pix + 1).start()

    def arrived(slot, place, sem):
        sending(place.at[slot], place, slot, sem.at[slot], sem, mate(0, 1)).wait_recv()

    @pl.when(not_first)
    def _():
        to_strip(1, pix - 1).wait_recv()

    @pl.when(not_last)
    def _():
        to_strip(0, pix + 1).wait_recv()

    @pl.when(jnp.logical_not(not_first))
    def _():
        from_strips[0] = jnp.zeros((32, COLS), BF)

    @pl.when(jnp.logical_not(not_last))
    def _():
        from_strips[1] = jnp.zeros((32, COLS), BF)

    rows = jnp.concatenate([from_strips[edge].astype(F32)[:EDGE] for edge in range(2)], axis=0)
    halos[pj] = rows.astype(BF)
    far_halo = sending(halos.at[pj], halos, MATES + core, halo_send.at[0], halo_recv, far_target)
    far_halo.start()
    sent.append(far_halo)
    send_to_mates(halos.at[pj], halos, halo_send, halo_recv)

    def not_handed(slot):
        return jnp.logical_or(corner, both(corner_mate, slot == 0))

    def hand_over(i, place, send_sem, recv_sem):
        slot = 2 * lax.rem(chip + i, 4) + core
        return slot, sending(place.at[slot], place, slot, send_sem.at[i], recv_sem, mate(0, 1))

    def hand_all_over(place, send_sem, recv_sem):
        for i in range(1, 4):
            slot, copy = hand_over(i, place, send_sem, recv_sem)

            @pl.when(jnp.logical_not(not_handed(slot)))
            def _():
                arrived(slot, place, recv_sem)
                send(copy, jnp.logical_not(sibling))

    hand_all_over(blocks, pass_send, block_recv)

    @pl.when(corner_strip)
    def _():
        pl.semaphore_wait(late, 1)
        to_strip(0, pix - 1).start()

    def to_corner(slot, place, sem, send_sem):
        return sending(place.at[slot], place, slot, send_sem, sem, {"pj": 0})

    def serve_corner():
        pl.semaphore_wait(late, 1)
        sending(own, blocks, pj, block_send.at[4], block_recv, {"pj": 0}).start()
        sending(halos.at[pj], halos, pj, halo_send.at[4], halo_recv, {"pj": 0}).start()
        for i in range(1, 4):
            hand_over(i, blocks, pass_send, block_recv)[1].start()
            to_corner(2 * i, blocks, block_recv, pass_send.at[3 + i]).start()

    def take(group):
        def one(half, _):
            slot = group * 2 + half

            @pl.when(slot != pj)
            def _():
                @pl.when(jnp.logical_or(not_handed(slot), jnp.logical_or(half != core, group == MATES // 2)))
                def _():
                    arrived(slot, blocks, block_recv)

                spread_image(blocks.at[slot], table, group, half)

            return 0

        lax.fori_loop(0, 2, one, 0)
        inner_scale(table, scale, group, band)

    def group_at(i):
        ahead = lax.rem(chip + i + number(both(corner_mate, chip == 0)), 4)
        return jnp.where(chip < 2, ahead, jnp.where(both(chip == 2, i < 2), 2 + i, 3 - i))

    second = jnp.where(far, MATES // 2, lax.rem(pj, 4))

    def early(i, _):
        take(group_at(i))
        return 0

    def pairs(i):
        group = group_at(i)
        for s in range(8):
            inner_rows(group, s, second, table, scale, stage, inside, band)

    lax.fori_loop(0, 4 - number(corner_mate), early, 0)

    @pl.when(sibling)
    def _():
        serve_corner()

    @pl.when(far)
    def _():
        take(second)

    pairs(0)
    pairs(1)
    hand_all_over(halos, pass_halo, halo_recv)
    pairs(2)

    @pl.when(corner_mate)
    def _():
        take(group_at(3))

    pairs(3)

    def halo_in(slot, _):
        @pl.when(slot != pj)
        def _():
            @pl.when(jnp.logical_or(not_handed(slot), jnp.logical_or(lax.rem(slot, 2) != core, slot >= MATES)))
            def _():
                arrived(slot, halos, halo_recv)

            @pl.when(both(sibling, slot > 1))
            def _():
                to_corner(slot, halos, halo_recv, hand_send.at[slot]).start()

        return 0

    lax.fori_loop(0, jnp.where(far, MATES + 2, MATES), halo_in, 0)
    for copy in sent:
        copy.wait_send()

    @pl.when(corner)
    def _():
        for copy in sent_by_corner:
            copy.wait_send()

    @pl.when(jnp.logical_not(corner))
    def _():
        for i in range(1, 4):
            slot, copy = hand_over(i, blocks, pass_send, block_recv)
            pl.when(jnp.logical_not(both(corner_mate, slot == 0)))(copy.wait_send)

    @pl.when(jnp.logical_not(jnp.logical_or(corner, sibling)))
    def _():
        for i in range(1, 4):
            slot, copy = hand_over(i, halos, pass_halo, halo_recv)
            pl.when(jnp.logical_not(both(corner_mate, slot == 0)))(copy.wait_send)

    @pl.when(sibling)
    def _():
        for i in range(1, 4):
            to_corner(2 * i, blocks, block_recv, pass_send.at[3 + i]).wait_send()
        for slot in range(2, MATES):
            to_corner(slot, halos, halo_recv, hand_send.at[slot]).wait_send()

    @pl.when(not_first)
    def _():
        to_strip(0, pix - 1).wait_send()

    @pl.when(not_last)
    def _():
        to_strip(1, pix + 1).wait_send()


def edge_kernel(table, halos, inner, stage, inside, result, margin, scale, edge_stage, out, out_sem):
    pi, pj = lax.axis_index("pi"), lax.axis_index("pj")
    far = (pj // 4) != pi
    second = jnp.where(far, MATES // 2, lax.rem(pj, 4))
    band = band_matrix()

    def take(group, source):
        for half in range(2):
            spread_halo(halos.at[source * 2 + half], margin, group, half)
        outer_scale(table, margin, scale, group, source, band)

    def write(group):
        return pltpu.make_async_copy(
            out.at[pl.ds(group * 8, 8)], result.at[pl.ds(group * 8, 8)], out_sem.at[group])

    take(4, second)
    for group in range(4):
        take(group, group)
        for s in range(8):
            outer_rows(group, s, margin, scale, stage, inside, edge_stage.at[group * 8 + s], out, band)
        write(group).start()
    for group in range(4):
        write(group).wait()


def second_call(*kept):
    on_chip = pl.BlockSpec(memory_space=pltpu.VMEM)
    return pl.pallas_call(
        edge_kernel,
        out_shape=jax.ShapeDtypeStruct((32, 8, STRIP, COLS), BF),
        in_specs=[on_chip] * 5,
        out_specs=pl.BlockSpec(memory_space=pltpu.HBM),
        scratch_shapes=[
            pltpu.VMEM((5 * 2 * 6 * 8, COLS), F32),
            pltpu.VMEM((5 * 6 * 8, COLS), F32),
            pltpu.VMEM((32, 64, COLS), F32),
            pltpu.VMEM((32, 8, STRIP, COLS), BF),
            pltpu.SemaphoreType.DMA((4,)),
        ],
        compiler_params=pltpu.CompilerParams(vmem_limit_bytes=16 << 20),
        name="coherence_edges",
    )(*kept)


def per_device(images):
    on_chip = pl.BlockSpec(memory_space=pltpu.VMEM)
    kept = pl.pallas_call(
        gather_kernel,
        out_shape=(
            pltpu.VMEM((5 * 2 * STRIP * 8, COLS), F32),
            pltpu.VMEM((MATES + 2, 2 * EDGE, COLS), BF),
            pltpu.VMEM((5 * INNER * 8, COLS), F32),
            pltpu.VMEM((32 * 8 * STRIP, COLS), F32),
            pltpu.VMEM((32 * 12 * 8, COLS), F32),
        ),
        in_specs=[pl.BlockSpec(memory_space=pltpu.HBM)],
        out_specs=(on_chip,) * 5,
        scratch_shapes=[
            pltpu.VMEM((2, 4, 16, COLS), BF),
            pltpu.VMEM((MATES + 2, 2, 4, 16, COLS), BF),
            pltpu.VMEM((2, 32, COLS), BF),
            pltpu.VMEM((2, 32, COLS), BF),
            pltpu.VMEM((2, 32, COLS), F32),
            pltpu.SemaphoreType.REGULAR,
            pltpu.SemaphoreType.REGULAR,
            pltpu.SemaphoreType.REGULAR,
            pltpu.SemaphoreType.DMA,
            pltpu.SemaphoreType.DMA((2,)),
            pltpu.SemaphoreType.DMA((2,)),
            pltpu.SemaphoreType.DMA((8,)),
            pltpu.SemaphoreType.DMA((MATES + 2,)),
            pltpu.SemaphoreType.DMA((7,)),
            pltpu.SemaphoreType.DMA((8,)),
            pltpu.SemaphoreType.DMA((MATES + 2,)),
            pltpu.SemaphoreType.DMA((MATES,)),
            pltpu.SemaphoreType.DMA((4,)),
        ],
        compiler_params=pltpu.CompilerParams(
            collective_id=0, has_side_effects=True, vmem_limit_bytes=16 << 20
        ),
        name="coherence_inner",
    )(pltpu.with_memory_space_constraint(images, pltpu.HBM))
    return second_call(*kept)


def solution(mesh):
    return jax.shard_map(
        per_device,
        mesh=mesh,
        in_specs=(P(None, ("pi", "pj"), "pix", None),),
        out_specs=P("pi", "pj", "pix", None),
        check_vma=False,
    )
```

```python
import jax
import jax.numpy as jnp
from jax import lax
from jax.experimental import pallas as pl
from jax.experimental.pallas import tpu as pltpu
from jax.sharding import PartitionSpec as P

BF = jnp.bfloat16
F32 = jnp.float32
MESH = pl.DeviceIdType.MESH
STRIP = 16
INNER = 10
COLS = 128
MATES = 8
EDGE = 24


def table_row(group, part, row):
    return ((group * 2 + part) * STRIP + row) * 8


def margin_row(group, part, row):
    return ((group * 2 + part) * 6 + row) * 8


def inner_sums(x):
    pairs = {j: x[j] + x[j + 1] for j in range(1, 15, 2)}
    full = []
    for s in range(0, 10, 2):
        middle = pairs[s + 1] + pairs[s + 3] + pairs[s + 5]
        full.append(x[s] + middle)
        full.append(middle + x[s + 7])
    first = (x[0] + pairs[1]) + x[3]
    second = first + x[4]
    last = (x[12] + pairs[13]) + x[15]
    before = x[11] + last
    return full, [first, second, second + x[5], x[10] + before, before, last]


def outer_sums(inside, x):
    above, below = x[1] + x[2], x[3] + x[4]
    return [
        inside[0] + (x[0] + above), inside[1] + above, inside[2] + x[2],
        inside[3] + x[3], inside[4] + below, inside[5] + (below + x[5]),
    ]


def sum_columns(rows, band):
    x = jnp.concatenate(rows, axis=0)
    high = x.astype(BF)
    low = (x - high.astype(F32)).astype(BF)
    return jnp.dot(jnp.concatenate([high, low], axis=1), band, preferred_element_type=F32)


def band_matrix():
    r = lax.broadcasted_iota(jnp.int32, (COLS, COLS), 0)
    c = lax.broadcasted_iota(jnp.int32, (COLS, COLS), 1)
    band = jnp.where(jnp.abs(r - c) <= 3, 1.0, 0.0).astype(BF)
    return jnp.concatenate([band, band], axis=0)


def spread_image(block, table, group, half):
    for part in range(2):
        for p in range(4):
            rows = block[part, p].astype(F32)
            for j in range(2):
                start = table_row(group, part, 8 * j) + half * 4 + p
                table[pl.ds(start, 8, stride=8), :] = rows[8 * j : 8 * j + 8]


def spread_halo(halo, margin, group, half):
    rows = halo[...].astype(F32)
    for edge in range(2):
        for part in range(2):
            for k in range(3):
                start = margin_row(group, part, 3 * edge + k) + half * 4
                first = EDGE * edge + (part * 3 + k) * 4
                margin[pl.ds(start, 4), :] = rows[first : first + 4]


def powers(load, rows):
    out = []
    for row in rows:
        a, b = load(0, row), load(1, row)
        out.append(a * a + b * b)
    return out


def products(first, second, rows):
    real, imag = [], []
    for row in rows:
        a = jnp.broadcast_to(first(0, row), (8, COLS))
        b = jnp.broadcast_to(first(1, row), (8, COLS))
        c, d = second(0, row), second(1, row)
        real.append(a * c + b * d)
        imag.append(b * c - a * d)
    return real, imag


def magnitude(x, y, first, second):
    q = x * x + y * y
    return (q * lax.rsqrt(jnp.maximum(q, 1e-36))) * (jnp.broadcast_to(first, (8, COLS)) * second)


def inner_scale(table, scale, group, band):
    full, _ = inner_sums(powers(lambda part, row: table[pl.ds(table_row(group, part, row), 8), :], range(STRIP)))
    scale[pl.ds(group * 8 * INNER, 8 * INNER), :] = lax.rsqrt(sum_columns(full, band))


def outer_scale(table, margin, scale, group, source, band):
    x = powers(lambda part, row: table[pl.ds(table_row(source, part, row), 8), :], range(STRIP))
    y = powers(lambda part, row: margin[pl.ds(margin_row(group, part, row), 8), :], range(6))
    scale[pl.ds(group * 8 * 6, 8 * 6), :] = lax.rsqrt(sum_columns(outer_sums(inner_sums(x)[1], y), band))


def inner_rows(group, s, second, table, scale, stage, inside, band):
    m = group * 8 + s
    real, imag = products(
        lambda part, row: table[pl.ds(table_row(group, part, row) + s, 1), :],
        lambda part, row: table[pl.ds(table_row(second, part, row), 8), :],
        range(STRIP),
    )
    real, real_inside = inner_sums(real)
    imag, imag_inside = inner_sums(imag)
    for i, value in enumerate(real_inside + imag_inside):
        inside[pl.ds((m * 12 + i) * 8, 8), :] = value
    w = sum_columns(real + imag, band)
    for r in range(INNER):
        value = magnitude(
            w[r * 8 : r * 8 + 8],
            w[(INNER + r) * 8 : (INNER + r) * 8 + 8],
            scale[pl.ds((group * INNER + r) * 8 + s, 1), :],
            scale[pl.ds((second * INNER + r) * 8, 8), :],
        )
        stage[pl.ds(m * 8 * STRIP + 3 + r, 8, stride=STRIP), :] = value


def outer_rows(group, s, margin, scale, stage, inside, edge_stage, out, band):
    m = group * 8 + s
    real, imag = products(
        lambda part, row: margin[pl.ds(margin_row(group, part, row) + s, 1), :],
        lambda part, row: margin[pl.ds(margin_row(4, part, row), 8), :],
        range(6),
    )
    kept = [inside[pl.ds((m * 12 + i) * 8, 8), :] for i in range(12)]
    w = sum_columns(outer_sums(kept[:6], real) + outer_sums(kept[6:], imag), band)
    for i, r in enumerate((0, 1, 2, 5, 6, 7)):
        value = magnitude(
            w[i * 8 : i * 8 + 8],
            w[(6 + i) * 8 : (6 + i) * 8 + 8],
            scale[pl.ds((group * 6 + i) * 8 + s, 1), :],
            scale[pl.ds((4 * 6 + i) * 8, 8), :],
        )
        edge_stage[pl.ds(r, 8, stride=8), :] = value
    row = lax.broadcasted_iota(jnp.int32, (8, COLS), 0)
    for n in range(8):
        edge = edge_stage[pl.ds(n * 8, 8), :]
        start = (m * 8 + n) * STRIP
        top = jnp.where(row < 3, edge, stage[pl.ds(start, 8), :])
        bottom = jnp.where(row > 4, edge, stage[pl.ds(start + 8, 8), :])
        out[m, n] = jnp.concatenate([top, bottom], axis=0).astype(BF)


def gather_kernel(images, table, halos, scale, stage, inside, own, blocks, edges, from_strips, edge_rows,
                  ready, late, next_ready, own_sem, pix_send, pix_recv, block_send, block_recv, pass_send, halo_send, halo_recv,
                  hand_send, pass_halo):
    pi, pj, pix = lax.axis_index("pi"), lax.axis_index("pj"), lax.axis_index("pix")
    last = lax.axis_size("pix") - 1
    chip, core = pj // 2, lax.rem(pj, 2)
    far = (pj // 4) != pi
    upper = pi == 1
    lower = jnp.logical_not(upper)
    not_first, not_last = pix > 0, pix < last

    def both(a, b):
        return jnp.logical_and(a, b)

    first_column = both(lower, pix == 0)
    corner = both(first_column, pj == 0)
    corner_mate = both(first_column, pj != 0)
    sibling = both(first_column, pj == 1)
    corner_strip = both(lower, both(pix == 1, pj == 0))
    corner_far = both(upper, both(pix == 0, pj == 0))

    before_step = both(not_last, both(upper, lax.rem(pix, 4) != 3))
    after_step = both(not_first, both(upper, lax.rem(pix, 4) != 0))

    def number(condition):
        return condition.astype(jnp.int32)

    def mate(chips, cores=0):
        return {"pj": 2 * lax.rem(chip + chips, 4) + lax.rem(core + cores, 2)}

    mates = [mate(3, 0), mate(3, 1), mate(2, 0), mate(2, 1), mate(1, 0), mate(1, 1), mate(0, 1)]
    far_target = {"pi": 1 - pi, "pj": 4 * pi + chip}
    far_sources = [{"pi": 1 - pi, "pj": 2 * lax.rem(pj, 4) + c} for c in range(2)]

    fetch = pltpu.make_async_copy(images, own, own_sem)
    fetch.start()
    barrier = pltpu.get_barrier_semaphore()

    def greet(device):
        pl.semaphore_signal(barrier, inc=1, device_id=device, device_id_type=MESH)

    @pl.when(jnp.logical_not(corner))
    def _():
        @pl.when(lower)
        def _():
            greet(far_target)

            @pl.when(far)
            def _():
                for device in far_sources:
                    greet(device)

        for device in mates:
            greet(device)

        @pl.when(corner_far)
        def _():
            greet(far_sources[0])

        @pl.when(both(not_first, jnp.logical_not(after_step)))
        def _():
            greet({"pix": pix - 1})

        @pl.when(not_last)
        def _():
            greet({"pix": pix + 1})

    band = band_matrix()

    def prepare():
        spread_image(own, table, chip, core)
        edge_rows[...] = jnp.zeros_like(edge_rows)
        for edge in range(2):
            for part in range(2):
                for k in range(3):
                    start = table_row(chip, part, (0 if edge == 0 else 13) + k) + core * 4
                    edge_rows[edge, pl.ds((part * 3 + k) * 4, 4), :] = table[pl.ds(start, 4), :]
        edges[...] = edge_rows[...].astype(BF)

    @pl.when(jnp.logical_not(corner))
    def _():
        fetch.wait()
        prepare()

    from_lower = jnp.where(upper, jnp.where(far, 3, 1), 0)
    greetings = MATES - 1 + number(not_first) + number(not_last) + from_lower
    pl.semaphore_wait(
        barrier, greetings + number(corner) - number(corner_mate) - number(corner_strip) - number(corner_far)
        - number(before_step))

    @pl.when(both(upper, far))
    def _():
        @pl.when(jnp.logical_not(corner_far))
        def _():
            pl.semaphore_signal(ready, inc=1, device_id=far_sources[0], device_id_type=MESH)

        pl.semaphore_signal(ready, inc=1, device_id=far_sources[1], device_id_type=MESH)

    @pl.when(after_step)
    def _():
        pl.semaphore_signal(next_ready, inc=1, device_id={"pix": pix - 1}, device_id_type=MESH)

    @pl.when(corner)
    def _():
        for device in ({"pj": 1}, {"pix": 1}):
            pl.semaphore_signal(late, inc=1, device_id=device, device_id_type=MESH)

    def to_strip(edge, strip):
        return pltpu.make_async_remote_copy(
            src_ref=edges.at[edge], dst_ref=from_strips.at[1 - edge], send_sem=pix_send.at[edge],
            recv_sem=pix_recv.at[1 - edge], device_id={"pix": strip}, device_id_type=MESH)

    def sending(source, place, slot, send_sem, recv_sem, device):
        return pltpu.make_async_remote_copy(
            src_ref=source, dst_ref=place.at[slot], send_sem=send_sem,
            recv_sem=recv_sem.at[slot], device_id=device, device_id_type=MESH)

    sent, sent_to_both = [], []

    def is_corner(device):
        return both(corner_mate, device["pj"] == 0)

    def send(copy, condition):
        @pl.when(condition)
        def _():
            copy.start()

    def send_to_mates(source, place, send_sem, recv_sem, to_both_cores):
        for i, device in enumerate((mate(3), mate(2), mate(1), mate(0, 1))):
            target = jnp.where(both(is_corner(device), pj != 1), 1, device["pj"])
            copy = sending(source, place, pj, send_sem.at[1 + i], recv_sem, {"pj": target})
            send(copy, jnp.logical_not(both(sibling, target == 0)))
            sent.append(copy)
        for i in range(1, 4):
            copy = sending(source, place, pj, send_sem.at[4 + i], recv_sem, mate(i, 1))
            send(copy, to_both_cores)
            sent_to_both.append((copy, to_both_cores))

    to_far = sending(own, blocks, MATES + core, block_send.at[0], block_recv, far_target)
    sent.append(to_far)

    @pl.when(corner)
    def _():
        fetch.wait()

    @pl.when(jnp.logical_or(upper, corner))
    def _():
        to_far.start()

    send_to_mates(own, blocks, block_send, block_recv, corner)

    @pl.when(corner)
    def _():
        prepare()

    @pl.when(both(not_first, jnp.logical_not(corner_strip)))
    def _():
        to_strip(0, pix - 1).start()

    @pl.when(both(not_last, jnp.logical_not(before_step)))
    def _():
        to_strip(1, pix + 1).start()

    @pl.when(both(lower, jnp.logical_not(corner)))
    def _():
        pl.semaphore_wait(ready, 1)
        to_far.start()

    @pl.when(before_step)
    def _():
        pl.semaphore_wait(next_ready, 1)
        to_strip(1, pix + 1).start()

    def arrived(slot, place, sem):
        sending(place.at[slot], place, slot, sem.at[slot], sem, mate(0, 1)).wait_recv()

    @pl.when(not_first)
    def _():
        to_strip(1, pix - 1).wait_recv()

    @pl.when(not_last)
    def _():
        to_strip(0, pix + 1).wait_recv()

    @pl.when(jnp.logical_not(not_first))
    def _():
        from_strips[0] = jnp.zeros((32, COLS), BF)

    @pl.when(jnp.logical_not(not_last))
    def _():
        from_strips[1] = jnp.zeros((32, COLS), BF)

    rows = jnp.concatenate([from_strips[edge].astype(F32)[:EDGE] for edge in range(2)], axis=0)
    halos[pj] = rows.astype(BF)
    far_halo = sending(halos.at[pj], halos, MATES + core, halo_send.at[0], halo_recv, far_target)
    far_halo.start()
    sent.append(far_halo)
    send_to_mates(halos.at[pj], halos, halo_send, halo_recv, jnp.logical_or(corner, upper))

    def not_handed(slot):
        return jnp.logical_or(corner, both(corner_mate, slot == 0))

    def hand_over(i, place, send_sem, recv_sem):
        slot = 2 * lax.rem(chip + i, 4) + core
        return slot, sending(place.at[slot], place, slot, send_sem.at[i], recv_sem, mate(0, 1))

    def hand_all_over(place, send_sem, recv_sem):
        for i in range(1, 4):
            slot, copy = hand_over(i, place, send_sem, recv_sem)

            @pl.when(jnp.logical_not(not_handed(slot)))
            def _():
                arrived(slot, place, recv_sem)
                send(copy, jnp.logical_not(sibling))

    hand_all_over(blocks, pass_send, block_recv)

    @pl.when(corner_strip)
    def _():
        pl.semaphore_wait(late, 1)
        to_strip(0, pix - 1).start()

    def to_corner(slot, place, sem, send_sem):
        return sending(place.at[slot], place, slot, send_sem, sem, {"pj": 0})

    def serve_corner():
        pl.semaphore_wait(late, 1)
        sending(own, blocks, pj, block_send.at[4], block_recv, {"pj": 0}).start()
        sending(halos.at[pj], halos, pj, halo_send.at[4], halo_recv, {"pj": 0}).start()
        for i in range(1, 4):
            hand_over(i, blocks, pass_send, block_recv)[1].start()
            to_corner(2 * i, blocks, block_recv, pass_send.at[3 + i]).start()

    def take(group):
        def one(half, _):
            slot = group * 2 + half

            @pl.when(slot != pj)
            def _():
                @pl.when(jnp.logical_or(not_handed(slot), jnp.logical_or(half != core, group == MATES // 2)))
                def _():
                    arrived(slot, blocks, block_recv)

                spread_image(blocks.at[slot], table, group, half)

            return 0

        lax.fori_loop(0, 2, one, 0)
        inner_scale(table, scale, group, band)

    def group_at(i):
        ahead = lax.rem(chip + i + number(both(corner_mate, chip == 0)), 4)
        return jnp.where(chip < 2, ahead, jnp.where(both(chip == 2, i < 2), 2 + i, 3 - i))

    second = jnp.where(far, MATES // 2, lax.rem(pj, 4))

    def early(i, _):
        take(group_at(i))
        return 0

    def pairs(i):
        group = group_at(i)
        for s in range(8):
            inner_rows(group, s, second, table, scale, stage, inside, band)

    lax.fori_loop(0, 4 - number(corner_mate), early, 0)

    @pl.when(sibling)
    def _():
        serve_corner()

    @pl.when(far)
    def _():
        take(second)

    pairs(0)
    pairs(1)

    @pl.when(jnp.logical_not(upper))
    def _():
        hand_all_over(halos, pass_halo, halo_recv)

    pairs(2)

    @pl.when(corner_mate)
    def _():
        take(group_at(3))

    pairs(3)

    def halo_in(slot, _):
        @pl.when(slot != pj)
        def _():
            @pl.when(jnp.logical_or(jnp.logical_or(upper, not_handed(slot)), jnp.logical_or(lax.rem(slot, 2) != core, slot >= MATES)))
            def _():
                arrived(slot, halos, halo_recv)

            @pl.when(both(sibling, slot > 1))
            def _():
                to_corner(slot, halos, halo_recv, hand_send.at[slot]).start()

        return 0

    lax.fori_loop(0, jnp.where(far, MATES + 2, MATES), halo_in, 0)
    for copy in sent:
        copy.wait_send()

    for copy, condition in sent_to_both:
        pl.when(condition)(copy.wait_send)

    @pl.when(jnp.logical_not(corner))
    def _():
        for i in range(1, 4):
            slot, copy = hand_over(i, blocks, pass_send, block_recv)
            pl.when(jnp.logical_not(both(corner_mate, slot == 0)))(copy.wait_send)

    @pl.when(jnp.logical_not(jnp.logical_or(upper, jnp.logical_or(corner, sibling))))
    def _():
        for i in range(1, 4):
            slot, copy = hand_over(i, halos, pass_halo, halo_recv)
            pl.when(jnp.logical_not(both(corner_mate, slot == 0)))(copy.wait_send)

    @pl.when(sibling)
    def _():
        for i in range(1, 4):
            to_corner(2 * i, blocks, block_recv, pass_send.at[3 + i]).wait_send()
        for slot in range(2, MATES):
            to_corner(slot, halos, halo_recv, hand_send.at[slot]).wait_send()

    @pl.when(not_first)
    def _():
        to_strip(0, pix - 1).wait_send()

    @pl.when(not_last)
    def _():
        to_strip(1, pix + 1).wait_send()


def edge_kernel(table, halos, inner, stage, inside, result, margin, scale, edge_stage, out, out_sem):
    pi, pj = lax.axis_index("pi"), lax.axis_index("pj")
    far = (pj // 4) != pi
    second = jnp.where(far, MATES // 2, lax.rem(pj, 4))
    band = band_matrix()

    def take(group, source):
        for half in range(2):
            spread_halo(halos.at[source * 2 + half], margin, group, half)
        outer_scale(table, margin, scale, group, source, band)

    def write(part):
        return pltpu.make_async_copy(
            out.at[pl.ds(part * 4, 4)], result.at[pl.ds(part * 4, 4)], out_sem.at[part])

    take(4, second)
    for group in range(4):
        take(group, group)
        for s in range(8):
            outer_rows(group, s, margin, scale, stage, inside, edge_stage.at[group * 8 + s], out, band)
            if s % 4 == 3:
                write(group * 2 + s // 4).start()
    for part in range(8):
        write(part).wait()


def second_call(*kept):
    on_chip = pl.BlockSpec(memory_space=pltpu.VMEM)
    return pl.pallas_call(
        edge_kernel,
        out_shape=jax.ShapeDtypeStruct((32, 8, STRIP, COLS), BF),
        in_specs=[on_chip] * 5,
        out_specs=pl.BlockSpec(memory_space=pltpu.HBM),
        scratch_shapes=[
            pltpu.VMEM((5 * 2 * 6 * 8, COLS), F32),
            pltpu.VMEM((5 * 6 * 8, COLS), F32),
            pltpu.VMEM((32, 64, COLS), F32),
            pltpu.VMEM((32, 8, STRIP, COLS), BF),
            pltpu.SemaphoreType.DMA((8,)),
        ],
        compiler_params=pltpu.CompilerParams(vmem_limit_bytes=16 << 20),
        name="coherence_edges",
    )(*kept)


def per_device(images):
    on_chip = pl.BlockSpec(memory_space=pltpu.VMEM)
    kept = pl.pallas_call(
        gather_kernel,
        out_shape=(
            pltpu.VMEM((5 * 2 * STRIP * 8, COLS), F32),
            pltpu.VMEM((MATES + 2, 2 * EDGE, COLS), BF),
            pltpu.VMEM((5 * INNER * 8, COLS), F32),
            pltpu.VMEM((32 * 8 * STRIP, COLS), F32),
            pltpu.VMEM((32 * 12 * 8, COLS), F32),
        ),
        in_specs=[pl.BlockSpec(memory_space=pltpu.HBM)],
        out_specs=(on_chip,) * 5,
        scratch_shapes=[
            pltpu.VMEM((2, 4, 16, COLS), BF),
            pltpu.VMEM((MATES + 2, 2, 4, 16, COLS), BF),
            pltpu.VMEM((2, 32, COLS), BF),
            pltpu.VMEM((2, 32, COLS), BF),
            pltpu.VMEM((2, 32, COLS), F32),
            pltpu.SemaphoreType.REGULAR,
            pltpu.SemaphoreType.REGULAR,
            pltpu.SemaphoreType.REGULAR,
            pltpu.SemaphoreType.DMA,
            pltpu.SemaphoreType.DMA((2,)),
            pltpu.SemaphoreType.DMA((2,)),
            pltpu.SemaphoreType.DMA((8,)),
            pltpu.SemaphoreType.DMA((MATES + 2,)),
            pltpu.SemaphoreType.DMA((7,)),
            pltpu.SemaphoreType.DMA((8,)),
            pltpu.SemaphoreType.DMA((MATES + 2,)),
            pltpu.SemaphoreType.DMA((MATES,)),
            pltpu.SemaphoreType.DMA((4,)),
        ],
        compiler_params=pltpu.CompilerParams(
            collective_id=0, has_side_effects=True, vmem_limit_bytes=16 << 20
        ),
        name="coherence_inner",
    )(pltpu.with_memory_space_constraint(images, pltpu.HBM))
    return second_call(*kept)


def solution(mesh):
    return jax.shard_map(
        per_device,
        mesh=mesh,
        in_specs=(P(None, ("pi", "pj"), "pix", None),),
        out_specs=P("pi", "pj", "pix", None),
        check_vma=False,
    )
```

```python
import jax
import jax.numpy as jnp
from jax import lax
from jax.experimental import pallas as pl
from jax.experimental.pallas import tpu as pltpu
from jax.sharding import PartitionSpec as P

BF = jnp.bfloat16
F32 = jnp.float32
MESH = pl.DeviceIdType.MESH
STRIP = 16
INNER = 10
COLS = 128
MATES = 8
EDGE = 24


def table_row(group, part, row):
    return ((group * 2 + part) * STRIP + row) * 8


def margin_row(group, part, row):
    return ((group * 2 + part) * 6 + row) * 8


def inner_sums(x):
    pairs = {j: x[j] + x[j + 1] for j in range(1, 15, 2)}
    full = []
    for s in range(0, 10, 2):
        middle = pairs[s + 1] + pairs[s + 3] + pairs[s + 5]
        full.append(x[s] + middle)
        full.append(middle + x[s + 7])
    first = (x[0] + pairs[1]) + x[3]
    second = first + x[4]
    last = (x[12] + pairs[13]) + x[15]
    before = x[11] + last
    return full, [first, second, second + x[5], x[10] + before, before, last]


def outer_sums(inside, x):
    above, below = x[1] + x[2], x[3] + x[4]
    return [
        inside[0] + (x[0] + above), inside[1] + above, inside[2] + x[2],
        inside[3] + x[3], inside[4] + below, inside[5] + (below + x[5]),
    ]


def sum_columns(rows, band):
    x = jnp.concatenate(rows, axis=0)
    high = x.astype(BF)
    low = (x - high.astype(F32)).astype(BF)
    return jnp.dot(jnp.concatenate([high, low], axis=1), band, preferred_element_type=F32)


def band_matrix():
    r = lax.broadcasted_iota(jnp.int32, (COLS, COLS), 0)
    c = lax.broadcasted_iota(jnp.int32, (COLS, COLS), 1)
    band = jnp.where(jnp.abs(r - c) <= 3, 1.0, 0.0).astype(BF)
    return jnp.concatenate([band, band], axis=0)


def spread_image(block, table, group, half):
    for part in range(2):
        for p in range(4):
            rows = block[part, p].astype(F32)
            for j in range(2):
                start = table_row(group, part, 8 * j) + half * 4 + p
                table[pl.ds(start, 8, stride=8), :] = rows[8 * j : 8 * j + 8]


def spread_halo(halo, margin, group, half):
    rows = halo[...].astype(F32)
    for edge in range(2):
        for part in range(2):
            for k in range(3):
                start = margin_row(group, part, 3 * edge + k) + half * 4
                first = EDGE * edge + (part * 3 + k) * 4
                margin[pl.ds(start, 4), :] = rows[first : first + 4]


def powers(load, rows):
    out = []
    for row in rows:
        a, b = load(0, row), load(1, row)
        out.append(a * a + b * b)
    return out


def products(first, second, rows):
    real, imag = [], []
    for row in rows:
        a = jnp.broadcast_to(first(0, row), (8, COLS))
        b = jnp.broadcast_to(first(1, row), (8, COLS))
        c, d = second(0, row), second(1, row)
        real.append(a * c + b * d)
        imag.append(b * c - a * d)
    return real, imag


def magnitude(x, y, first, second):
    q = x * x + y * y
    return (q * lax.rsqrt(jnp.maximum(q, 1e-36))) * (jnp.broadcast_to(first, (8, COLS)) * second)


def inner_scale(table, scale, group, band):
    full, _ = inner_sums(powers(lambda part, row: table[pl.ds(table_row(group, part, row), 8), :], range(STRIP)))
    scale[pl.ds(group * 8 * INNER, 8 * INNER), :] = lax.rsqrt(sum_columns(full, band))


def outer_scale(table, margin, scale, group, source, band):
    x = powers(lambda part, row: table[pl.ds(table_row(source, part, row), 8), :], range(STRIP))
    y = powers(lambda part, row: margin[pl.ds(margin_row(group, part, row), 8), :], range(6))
    scale[pl.ds(group * 8 * 6, 8 * 6), :] = lax.rsqrt(sum_columns(outer_sums(inner_sums(x)[1], y), band))


def inner_rows(group, s, second, table, scale, stage, inside, band):
    m = group * 8 + s
    real, imag = products(
        lambda part, row: table[pl.ds(table_row(group, part, row) + s, 1), :],
        lambda part, row: table[pl.ds(table_row(second, part, row), 8), :],
        range(STRIP),
    )
    real, real_inside = inner_sums(real)
    imag, imag_inside = inner_sums(imag)
    for i, value in enumerate(real_inside + imag_inside):
        inside[pl.ds((m * 12 + i) * 8, 8), :] = value
    w = sum_columns(real + imag, band)
    for r in range(INNER):
        value = magnitude(
            w[r * 8 : r * 8 + 8],
            w[(INNER + r) * 8 : (INNER + r) * 8 + 8],
            scale[pl.ds((group * INNER + r) * 8 + s, 1), :],
            scale[pl.ds((second * INNER + r) * 8, 8), :],
        )
        stage[pl.ds(m * 8 * STRIP + 3 + r, 8, stride=STRIP), :] = value


def outer_rows(group, s, margin, scale, stage, inside, edge_stage, out, band):
    m = group * 8 + s
    real, imag = products(
        lambda part, row: margin[pl.ds(margin_row(group, part, row) + s, 1), :],
        lambda part, row: margin[pl.ds(margin_row(4, part, row), 8), :],
        range(6),
    )
    kept = [inside[pl.ds((m * 12 + i) * 8, 8), :] for i in range(12)]
    w = sum_columns(outer_sums(kept[:6], real) + outer_sums(kept[6:], imag), band)
    for i, r in enumerate((0, 1, 2, 5, 6, 7)):
        value = magnitude(
            w[i * 8 : i * 8 + 8],
            w[(6 + i) * 8 : (6 + i) * 8 + 8],
            scale[pl.ds((group * 6 + i) * 8 + s, 1), :],
            scale[pl.ds((4 * 6 + i) * 8, 8), :],
        )
        edge_stage[pl.ds(r, 8, stride=8), :] = value
    row = lax.broadcasted_iota(jnp.int32, (8, COLS), 0)
    for n in range(8):
        edge = edge_stage[pl.ds(n * 8, 8), :]
        start = (m * 8 + n) * STRIP
        top = jnp.where(row < 3, edge, stage[pl.ds(start, 8), :])
        bottom = jnp.where(row > 4, edge, stage[pl.ds(start + 8, 8), :])
        out[m, n] = jnp.concatenate([top, bottom], axis=0).astype(BF)


def gather_kernel(images, table, halos, scale, stage, inside, own, blocks, edges, from_strips, edge_rows,
                  ready, late, next_ready, own_sem, pix_send, pix_recv, block_send, block_recv, pass_send, halo_send, halo_recv,
                  hand_send, pass_halo):
    pi, pj, pix = lax.axis_index("pi"), lax.axis_index("pj"), lax.axis_index("pix")
    last = lax.axis_size("pix") - 1
    chip, core = pj // 2, lax.rem(pj, 2)
    far = (pj // 4) != pi
    upper = pi == 1
    lower = jnp.logical_not(upper)
    not_first, not_last = pix > 0, pix < last

    def both(a, b):
        return jnp.logical_and(a, b)

    first_column = both(lower, pix == 0)
    corner = both(first_column, pj == 0)
    corner_mate = both(first_column, pj != 0)
    sibling = both(first_column, pj == 1)
    corner_strip = both(lower, both(pix == 1, pj == 0))
    corner_far = both(upper, both(pix == 0, pj == 0))

    before_step = both(not_last, both(upper, lax.rem(pix, 4) != 3))
    after_step = both(not_first, both(upper, lax.rem(pix, 4) != 0))

    def number(condition):
        return condition.astype(jnp.int32)

    def mate(chips, cores=0):
        return {"pj": 2 * lax.rem(chip + chips, 4) + lax.rem(core + cores, 2)}

    mates = [mate(3, 0), mate(3, 1), mate(2, 0), mate(2, 1), mate(1, 0), mate(1, 1), mate(0, 1)]
    far_target = {"pi": 1 - pi, "pj": 4 * pi + chip}
    far_sources = [{"pi": 1 - pi, "pj": 2 * lax.rem(pj, 4) + c} for c in range(2)]

    fetch = pltpu.make_async_copy(images, own, own_sem)
    fetch.start()
    barrier = pltpu.get_barrier_semaphore()

    def greet(device):
        pl.semaphore_signal(barrier, inc=1, device_id=device, device_id_type=MESH)

    @pl.when(jnp.logical_not(corner))
    def _():
        @pl.when(lower)
        def _():
            greet(far_target)

            @pl.when(far)
            def _():
                for device in far_sources:
                    greet(device)

        for device in mates:
            greet(device)

        @pl.when(corner_far)
        def _():
            greet(far_sources[0])

        @pl.when(both(not_first, jnp.logical_not(after_step)))
        def _():
            greet({"pix": pix - 1})

        @pl.when(not_last)
        def _():
            greet({"pix": pix + 1})

    band = band_matrix()

    def prepare():
        spread_image(own, table, chip, core)
        edge_rows[...] = jnp.zeros_like(edge_rows)
        for edge in range(2):
            for part in range(2):
                for k in range(3):
                    start = table_row(chip, part, (0 if edge == 0 else 13) + k) + core * 4
                    edge_rows[edge, pl.ds((part * 3 + k) * 4, 4), :] = table[pl.ds(start, 4), :]
        edges[...] = edge_rows[...].astype(BF)

    @pl.when(jnp.logical_not(corner))
    def _():
        fetch.wait()
        prepare()

    from_lower = jnp.where(upper, jnp.where(far, 3, 1), 0)
    greetings = MATES - 1 + number(not_first) + number(not_last) + from_lower
    pl.semaphore_wait(
        barrier, greetings + number(corner) - number(corner_mate) - number(corner_strip) - number(corner_far)
        - number(before_step))

    @pl.when(both(upper, far))
    def _():
        @pl.when(jnp.logical_not(corner_far))
        def _():
            pl.semaphore_signal(ready, inc=1, device_id=far_sources[0], device_id_type=MESH)

        pl.semaphore_signal(ready, inc=1, device_id=far_sources[1], device_id_type=MESH)

    @pl.when(after_step)
    def _():
        pl.semaphore_signal(next_ready, inc=1, device_id={"pix": pix - 1}, device_id_type=MESH)

    @pl.when(corner)
    def _():
        for device in ({"pj": 1}, {"pix": 1}):
            pl.semaphore_signal(late, inc=1, device_id=device, device_id_type=MESH)

    def to_strip(edge, strip):
        return pltpu.make_async_remote_copy(
            src_ref=edges.at[edge], dst_ref=from_strips.at[1 - edge], send_sem=pix_send.at[edge],
            recv_sem=pix_recv.at[1 - edge], device_id={"pix": strip}, device_id_type=MESH)

    def sending(source, place, slot, send_sem, recv_sem, device):
        return pltpu.make_async_remote_copy(
            src_ref=source, dst_ref=place.at[slot], send_sem=send_sem,
            recv_sem=recv_sem.at[slot], device_id=device, device_id_type=MESH)

    sent, sent_to_both = [], []

    def is_corner(device):
        return both(corner_mate, device["pj"] == 0)

    def send(copy, condition):
        @pl.when(condition)
        def _():
            copy.start()

    def send_to_mates(source, place, send_sem, recv_sem, to_both_cores):
        for i, device in enumerate((mate(3), mate(2), mate(1), mate(0, 1))):
            target = jnp.where(both(is_corner(device), pj != 1), 1, device["pj"])
            copy = sending(source, place, pj, send_sem.at[1 + i], recv_sem, {"pj": target})
            send(copy, jnp.logical_not(both(sibling, target == 0)))
            sent.append(copy)
        for i in range(1, 4):
            copy = sending(source, place, pj, send_sem.at[4 + i], recv_sem, mate(i, 1))
            send(copy, to_both_cores)
            sent_to_both.append((copy, to_both_cores))

    to_far = sending(own, blocks, MATES + core, block_send.at[0], block_recv, far_target)
    sent.append(to_far)

    @pl.when(corner)
    def _():
        fetch.wait()

    @pl.when(jnp.logical_or(upper, corner))
    def _():
        to_far.start()

    send_to_mates(own, blocks, block_send, block_recv, corner)

    @pl.when(corner)
    def _():
        prepare()

    @pl.when(both(not_first, jnp.logical_not(corner_strip)))
    def _():
        to_strip(0, pix - 1).start()

    @pl.when(both(not_last, jnp.logical_not(before_step)))
    def _():
        to_strip(1, pix + 1).start()

    @pl.when(both(lower, jnp.logical_not(corner)))
    def _():
        pl.semaphore_wait(ready, 1)
        to_far.start()

    @pl.when(before_step)
    def _():
        pl.semaphore_wait(next_ready, 1)
        to_strip(1, pix + 1).start()

    def arrived(slot, place, sem):
        sending(place.at[slot], place, slot, sem.at[slot], sem, mate(0, 1)).wait_recv()

    @pl.when(not_first)
    def _():
        to_strip(1, pix - 1).wait_recv()

    @pl.when(not_last)
    def _():
        to_strip(0, pix + 1).wait_recv()

    @pl.when(jnp.logical_not(not_first))
    def _():
        from_strips[0] = jnp.zeros((32, COLS), BF)

    @pl.when(jnp.logical_not(not_last))
    def _():
        from_strips[1] = jnp.zeros((32, COLS), BF)

    rows = jnp.concatenate([from_strips[edge].astype(F32)[:EDGE] for edge in range(2)], axis=0)
    halos[pj] = rows.astype(BF)
    far_halo = sending(halos.at[pj], halos, MATES + core, halo_send.at[0], halo_recv, far_target)
    far_halo.start()
    sent.append(far_halo)
    send_to_mates(halos.at[pj], halos, halo_send, halo_recv, jnp.logical_or(corner, upper))

    def not_handed(slot):
        return jnp.logical_or(corner, both(corner_mate, slot == 0))

    def hand_over(i, place, send_sem, recv_sem):
        slot = 2 * lax.rem(chip + i, 4) + core
        return slot, sending(place.at[slot], place, slot, send_sem.at[i], recv_sem, mate(0, 1))

    def hand_all_over(place, send_sem, recv_sem):
        for i in range(1, 4):
            slot, copy = hand_over(i, place, send_sem, recv_sem)

            @pl.when(jnp.logical_not(not_handed(slot)))
            def _():
                arrived(slot, place, recv_sem)
                send(copy, jnp.logical_not(sibling))

    hand_all_over(blocks, pass_send, block_recv)

    @pl.when(corner_strip)
    def _():
        pl.semaphore_wait(late, 1)
        to_strip(0, pix - 1).start()

    def to_corner(slot, place, sem, send_sem):
        return sending(place.at[slot], place, slot, send_sem, sem, {"pj": 0})

    def serve_corner():
        pl.semaphore_wait(late, 1)
        sending(own, blocks, pj, block_send.at[4], block_recv, {"pj": 0}).start()
        sending(halos.at[pj], halos, pj, halo_send.at[4], halo_recv, {"pj": 0}).start()
        for i in range(1, 4):
            hand_over(i, blocks, pass_send, block_recv)[1].start()
            to_corner(2 * i, blocks, block_recv, pass_send.at[3 + i]).start()

    def take(group):
        def one(half, _):
            slot = group * 2 + half

            @pl.when(slot != pj)
            def _():
                @pl.when(jnp.logical_or(not_handed(slot), jnp.logical_or(half != core, group == MATES // 2)))
                def _():
                    arrived(slot, blocks, block_recv)

                spread_image(blocks.at[slot], table, group, half)

            return 0

        lax.fori_loop(0, 2, one, 0)
        inner_scale(table, scale, group, band)

    def group_at(i):
        ahead = lax.rem(chip + i + number(both(corner_mate, chip == 0)), 4)
        return jnp.where(chip < 2, ahead, jnp.where(both(chip == 2, i < 2), 2 + i, 3 - i))

    second = jnp.where(far, MATES // 2, lax.rem(pj, 4))

    def early(i, _):
        take(group_at(i))
        return 0

    def pairs(i):
        group = group_at(i)
        for s in range(8):
            inner_rows(group, s, second, table, scale, stage, inside, band)

    lax.fori_loop(0, 4 - number(corner_mate), early, 0)

    @pl.when(sibling)
    def _():
        serve_corner()

    @pl.when(far)
    def _():
        take(second)

    pairs(0)
    pairs(1)

    @pl.when(jnp.logical_not(upper))
    def _():
        hand_all_over(halos, pass_halo, halo_recv)

    pairs(2)

    @pl.when(corner_mate)
    def _():
        take(group_at(3))

    pairs(3)

    def halo_in(slot, _):
        @pl.when(slot != pj)
        def _():
            @pl.when(jnp.logical_or(jnp.logical_or(upper, not_handed(slot)), jnp.logical_or(lax.rem(slot, 2) != core, slot >= MATES)))
            def _():
                arrived(slot, halos, halo_recv)

            @pl.when(both(sibling, slot > 1))
            def _():
                to_corner(slot, halos, halo_recv, hand_send.at[slot]).start()

        return 0

    lax.fori_loop(0, jnp.where(far, MATES + 2, MATES), halo_in, 0)
    for copy in sent:
        copy.wait_send()

    for copy, condition in sent_to_both:
        pl.when(condition)(copy.wait_send)

    @pl.when(jnp.logical_not(corner))
    def _():
        for i in range(1, 4):
            slot, copy = hand_over(i, blocks, pass_send, block_recv)
            pl.when(jnp.logical_not(both(corner_mate, slot == 0)))(copy.wait_send)

    @pl.when(jnp.logical_not(jnp.logical_or(upper, jnp.logical_or(corner, sibling))))
    def _():
        for i in range(1, 4):
            slot, copy = hand_over(i, halos, pass_halo, halo_recv)
            pl.when(jnp.logical_not(both(corner_mate, slot == 0)))(copy.wait_send)

    @pl.when(sibling)
    def _():
        for i in range(1, 4):
            to_corner(2 * i, blocks, block_recv, pass_send.at[3 + i]).wait_send()
        for slot in range(2, MATES):
            to_corner(slot, halos, halo_recv, hand_send.at[slot]).wait_send()

    @pl.when(not_first)
    def _():
        to_strip(0, pix - 1).wait_send()

    @pl.when(not_last)
    def _():
        to_strip(1, pix + 1).wait_send()


def edge_kernel(table, halos, inner, stage, inside, result, margin, scale, edge_stage, out, out_sem):
    pi, pj = lax.axis_index("pi"), lax.axis_index("pj")
    far = (pj // 4) != pi
    second = jnp.where(far, MATES // 2, lax.rem(pj, 4))
    band = band_matrix()

    def take(group, source):
        for half in range(2):
            spread_halo(halos.at[source * 2 + half], margin, group, half)
        outer_scale(table, margin, scale, group, source, band)

    def write(part):
        return pltpu.make_async_copy(
            out.at[pl.ds(part * 4, 4)], result.at[pl.ds(part * 4, 4)], out_sem.at[part])

    take(4, second)
    for group in range(4):
        take(group, group)
        for s in range(8):
            outer_rows(group, s, margin, scale, stage, inside, edge_stage.at[group * 8 + s], out, band)
            if s % 4 == 3:
                write(group * 2 + s // 4).start()
    for part in range(8):
        write(part).wait()


def second_call(*kept):
    on_chip = pl.BlockSpec(memory_space=pltpu.VMEM)
    return pl.pallas_call(
        edge_kernel,
        out_shape=jax.ShapeDtypeStruct((32, 8, STRIP, COLS), BF),
        in_specs=[on_chip] * 5,
        out_specs=pl.BlockSpec(memory_space=pltpu.HBM),
        scratch_shapes=[
            pltpu.VMEM((5 * 2 * 6 * 8, COLS), F32),
            pltpu.VMEM((5 * 6 * 8, COLS), F32),
            pltpu.VMEM((32, 72, COLS), F32),
            pltpu.VMEM((32, 8, STRIP, COLS), BF),
            pltpu.SemaphoreType.DMA((8,)),
        ],
        compiler_params=pltpu.CompilerParams(vmem_limit_bytes=16 << 20),
        name="coherence_edges",
    )(*kept)


def per_device(images):
    on_chip = pl.BlockSpec(memory_space=pltpu.VMEM)
    kept = pl.pallas_call(
        gather_kernel,
        out_shape=(
            pltpu.VMEM((5 * 2 * STRIP * 8 + 64, COLS), F32),
            pltpu.VMEM((MATES + 2, 2 * EDGE, COLS), BF),
            pltpu.VMEM((5 * INNER * 8, COLS), F32),
            pltpu.VMEM((32 * 8 * STRIP + 128, COLS), F32),
            pltpu.VMEM((32 * 12 * 8, COLS), F32),
        ),
        in_specs=[pl.BlockSpec(memory_space=pltpu.HBM)],
        out_specs=(on_chip,) * 5,
        scratch_shapes=[
            pltpu.VMEM((2, 4, 16, COLS), BF),
            pltpu.VMEM((MATES + 2, 2, 4, 16, COLS), BF),
            pltpu.VMEM((2, 32, COLS), BF),
            pltpu.VMEM((2, 32, COLS), BF),
            pltpu.VMEM((2, 32, COLS), F32),
            pltpu.SemaphoreType.REGULAR,
            pltpu.SemaphoreType.REGULAR,
            pltpu.SemaphoreType.REGULAR,
            pltpu.SemaphoreType.DMA,
            pltpu.SemaphoreType.DMA((2,)),
            pltpu.SemaphoreType.DMA((2,)),
            pltpu.SemaphoreType.DMA((8,)),
            pltpu.SemaphoreType.DMA((MATES + 2,)),
            pltpu.SemaphoreType.DMA((7,)),
            pltpu.SemaphoreType.DMA((8,)),
            pltpu.SemaphoreType.DMA((MATES + 2,)),
            pltpu.SemaphoreType.DMA((MATES,)),
            pltpu.SemaphoreType.DMA((4,)),
        ],
        compiler_params=pltpu.CompilerParams(
            collective_id=0, has_side_effects=True, vmem_limit_bytes=16 << 20
        ),
        name="coherence_inner",
    )(pltpu.with_memory_space_constraint(images, pltpu.HBM))
    return second_call(*kept)


def solution(mesh):
    return jax.shard_map(
        per_device,
        mesh=mesh,
        in_specs=(P(None, ("pi", "pj"), "pix", None),),
        out_specs=P("pi", "pj", "pix", None),
        check_vma=False,
    )
```
